32 devices in a mesh: row: 8 (over y, x, core), col: 4 (over z).
Axes of the slice: x: 2, y: 2, z: 4, core: 2. Of those that a mesh axis runs over, the one named last changes fastest.
Arguments:
- record: bfloat16 [6, 2048, 2560], P(None, ('row', 'col')), may hold values from -6 to 6
- taps: float32 [200], replicated, may hold values from -0.4375 to 0.4375
- plan: int32 [6], replicated, may hold values from 0 to 5, each once
- quality: int32 [2048], P(('row', 'col')), may hold values 0 or 1
Outputs:
- correlation: float32 [51, 2048, 2048], P(None, 'row', 'col')
The draws below stay inside these ranges and needn't reach their ends.
Inputs may be any that keep to these rules, and one draw needn't show every extreme that they name: plan is a permutation of the recorded sub-windows; its first 4 entries name the ones that are stacked.
All inputs are finite; a program needn't handle non-finite values. No bound on the sum of `quality` on one device may be relied on, other than what follows from the above.
Results may differ from the reference program's by a relative error of at most 0.0039.
Values may be sent and summed in bfloat16 or wider, within the bound.
A program may use at most 128 MiB of HBM per device.

```python
import math
import jax
import jax.numpy as jnp
from jax import lax

C = 2048
STRIDE = 20
TAPS = 200
HALFWIN = 32
MAXLAG = 25
SUB = 4
SLOTS = 6
RAW = 2560
LAGS = 51


def place_ends(array, key, least, high):
    longest = array.shape.index(max(array.shape))
    spots = []
    for shift in (0, 1):
        where = [jax.random.randint(jax.random.fold_in(key, axis), (), 0, length) for axis, length in enumerate(array.shape)]
        where[longest] = (where[longest] + shift) % array.shape[longest]
        spots.append(tuple(where))
    return array.at[spots[0]].set(least).at[spots[1]].set(high)


def shard_levels(key, shape, shards, smallest, high):
    gain = 1.0
    for position, parts in shards:
        steps = jax.random.uniform(jax.random.fold_in(jax.random.fold_in(key, 6), position), (parts,), jnp.float32, smallest / len(shards), high / len(shards))
        gain = gain * jnp.repeat(jnp.exp(steps), shape[position] // parts).reshape((-1,) + (1,) * (len(shape) - 1 - position))
    return gain


def gaussian(stream_key, extent, deviation, bound, pieces=(), held_as=jnp.bfloat16):
    drawn = jax.random.normal(stream_key, extent, jnp.float32) * deviation
    if len(pieces) > 0:
        drawn = shard_levels(stream_key, extent, pieces, -0.22, 0.18) * drawn
    return jnp.clip(drawn, min=-bound, max=bound).astype(held_as)


def setup_inputs(seed: int = 0) -> dict:
    arg_keys = jax.random.split(jax.random.key(seed), 5)
    return {
        "record": gaussian(arg_keys[0], (SLOTS, C, RAW), 1.0, 6.0, ((1, 32),)),
        "taps": gaussian(arg_keys[1], (TAPS,), TAPS ** -0.5, 0.4375, (), jnp.float32),
        "plan": jax.random.permutation(arg_keys[2], SLOTS).astype(jnp.int32),
        "quality": place_ends((jax.random.randint(arg_keys[3], (C,), 0, 8) < 7).astype(jnp.int32), jax.random.fold_in(arg_keys[3], 1), 0, 1),
    }


def decimate(picked, taps):
    window_count, chan_count, raw_length = picked.shape
    frame_count = raw_length // STRIDE
    block_count = TAPS // STRIDE
    blocks = picked.astype(jnp.float32).reshape(window_count, chan_count, frame_count, STRIDE)
    blocks = jnp.pad(blocks, ((0, 0), (0, 0), (0, block_count - 1), (0, 0)))
    tap_table = taps.reshape(block_count, STRIDE)
    filtered = jnp.zeros((chan_count, window_count, frame_count), jnp.float32)
    for offset in range(block_count):
        filtered = filtered + jnp.einsum('sckr,r->csk', blocks[:, :, offset:offset + frame_count, :], tap_table[offset], precision=lax.Precision.HIGHEST)
    return filtered

def whiten(decimated, quality):
    frame_count = decimated.shape[2]
    places = jnp.arange(frame_count, dtype=jnp.int32)
    band_matrix = (jnp.abs(places[:, None] - places[None, :]) <= HALFWIN).astype(jnp.float32)
    envelope = jnp.einsum('csk,kj->csj', jnp.abs(decimated), band_matrix, precision=lax.Precision.HIGHEST) / (2 * HALFWIN + 1)
    scaled = decimated / (envelope + 1e-05) * quality.astype(jnp.float32)[:, None, None]
    return scaled.astype(jnp.bfloat16)

def correlate(source, receiver):
    source_count, window_count, frame_count = source.shape
    receiver_count = receiver.shape[0]
    flat_source = source.astype(jnp.float32).reshape(source_count, window_count * frame_count)
    padded = jnp.pad(receiver.astype(jnp.float32), ((0, 0), (0, 0), (MAXLAG, MAXLAG)))

    def one_lag(offset):
        moved = lax.dynamic_slice_in_dim(padded, offset, frame_count, 2).reshape(receiver_count, window_count * frame_count)
        return lax.dot_general(flat_source, moved, (((1,), (1,)), ((), ())), precision=lax.Precision.HIGHEST, preferred_element_type=jnp.float32)
    stacked = lax.map(one_lag, jnp.arange(LAGS, dtype=jnp.int32))
    return stacked * (1.0 / math.sqrt(window_count * frame_count))

def reference(record, taps, plan, quality):
    picked = jnp.take(record, plan[:SUB], axis=0)
    whitened = whiten(decimate(picked, taps), quality)
    return correlate(whitened, whitened)
```

```python
import functools
import math

import jax
import jax.numpy as jnp
from jax import lax
from jax.experimental import pallas as pl
from jax.experimental.pallas import tpu as pltpu
from jax.sharding import PartitionSpec as P

STRIDE = 20
TAPS = 200
HALFWIN = 32
MAXLAG = 25
SUB = 4
LAGS = 51
LANES = 128
BAND_FRAMES = 32
BAND_STEP = BAND_FRAMES * STRIDE
BAND_WIDTH = 896
PARTS = 3
LAG_GROUP = 3
SLOTS = 3

MESH = pl.DeviceIdType.MESH
NT = (((1,), (1,)), ((), ()))


def split_parts(values, count):
    parts = []
    for _ in range(count):
        part = values.astype(jnp.bfloat16)
        parts.append(part)
        values = values - part.astype(jnp.float32)
    return parts


def filter_band(tap_row):
    base = jnp.broadcast_to(tap_row, (8, TAPS))
    base = jnp.concatenate([base, jnp.zeros((8, BAND_WIDTH - TAPS), jnp.float32)], axis=1)
    place = lax.broadcasted_iota(jnp.int32, (8, BAND_WIDTH), 0)
    groups = []
    for group in range(BAND_FRAMES // 8):
        held = jnp.zeros((8, BAND_WIDTH), jnp.float32)
        for row in range(8):
            shift = (group * 8 + row) * STRIDE
            moved = base if shift == 0 else pltpu.roll(base, shift, 1)
            held = jnp.where(place == row, moved, held)
        groups.append(held)
    return jnp.concatenate(groups, axis=0)


def whiten_and_send(
    rows, cols, plan_ref, tap_ref, quality_ref, record_ref,
    source_ref, receiver_ref,
    raw, table, load_sem, source_sem, receiver_sem, out_sem, plane_sem, twin_sem,
):
    r, c = lax.axis_index("row"), lax.axis_index("col")
    parity = lax.rem(r, 2)
    pair = lax.div(r, 2)
    twin = r + 1 - 2 * parity
    on_diagonal = pair == c
    slots, chans, length = raw.shape
    frames = length // STRIDE

    loads = [
        pltpu.make_async_copy(record_ref.at[i], raw.at[i], load_sem.at[i]) for i in range(slots)
    ]
    for load in loads:
        load.start()

    barrier = pltpu.get_barrier_semaphore()

    def greet(row, col):
        pl.semaphore_signal(barrier, inc=1, device_id=(row, col), device_id_type=MESH)

    for step in range(1, cols):
        greet(r, lax.rem(c + step, cols))
        greet(lax.rem(r + 2 * step, rows), pair)
    greet(twin, c)

    @pl.when(jnp.logical_not(on_diagonal))
    def _():
        for step in range(1, cols):
            greet(2 * c + parity, lax.rem(pair + step, cols))

    table[...] = jnp.zeros_like(table)
    band = filter_band(tap_ref[...])
    for number, part in enumerate(split_parts(band, PARTS)):
        for block in range(frames // BAND_FRAMES):
            start = block * BAND_STEP
            width = min(BAND_WIDTH, length - start)
            first = number * frames + block * BAND_FRAMES
            table[first : first + BAND_FRAMES, start : start + width] = part[:, :width]

    for load in loads:
        load.wait()
    picked = jnp.concatenate([raw[plan_ref[s]] for s in range(SUB)], axis=0)
    summed = lax.dot_general(picked, table[...], NT, preferred_element_type=jnp.float32)
    decimated = summed[:, :frames]
    for number in range(1, PARTS):
        decimated = decimated + summed[:, number * frames : (number + 1) * frames]

    near = lax.broadcasted_iota(jnp.int32, (frames, frames), 0)
    near = jnp.abs(near - lax.broadcasted_iota(jnp.int32, (frames, frames), 1)) <= HALFWIN
    near = near.astype(jnp.float32).astype(jnp.bfloat16)
    envelope = jnp.zeros_like(decimated)
    for part in split_parts(jnp.abs(decimated), PARTS):
        envelope = envelope + jnp.dot(part, near, preferred_element_type=jnp.float32)
    envelope = envelope / (2 * HALFWIN + 1)
    square = lax.broadcasted_iota(jnp.int32, (chans, chans), 0) == lax.broadcasted_iota(
        jnp.int32, (chans, chans), 1
    )
    usable = jnp.broadcast_to(quality_ref[...].astype(jnp.float32), (chans, chans))
    usable = jnp.sum(jnp.where(square, usable, 0.0), axis=1, keepdims=True)
    scaled = decimated / (envelope + 1e-05)
    for s in range(SUB):
        window = scaled[s * chans : (s + 1) * chans] * usable
        source_ref[c, :, s * frames : (s + 1) * frames] = window.astype(jnp.bfloat16)

    @pl.when(on_diagonal)
    def _():
        pl.semaphore_wait(barrier, 2 * (cols - 1) + 1)

    @pl.when(jnp.logical_not(on_diagonal))
    def _():
        pl.semaphore_wait(barrier, 3 * (cols - 1) + 1)

    mine = source_ref.at[c]
    half = parity * cols

    def plane_copy(step):
        return pltpu.make_async_remote_copy(
            src_ref=mine,
            dst_ref=receiver_ref.at[half + c],
            send_sem=plane_sem.at[step],
            recv_sem=receiver_sem.at[half + c],
            device_id=(lax.rem(r + 2 * step, rows), pair),
            device_id_type=MESH,
        )

    def row_copy(step):
        return pltpu.make_async_remote_copy(
            src_ref=mine,
            dst_ref=source_ref.at[c],
            send_sem=out_sem.at[step],
            recv_sem=source_sem.at[c],
            device_id=(r, lax.rem(c + step, cols)),
            device_id_type=MESH,
        )

    for step in range(1, cols):
        row_copy(step).start()
        plane_copy(step).start()

    def source_arrival(number):
        return pltpu.make_async_remote_copy(
            src_ref=mine,
            dst_ref=source_ref.at[number],
            send_sem=out_sem.at[0],
            recv_sem=source_sem.at[number],
            device_id=(r, lax.rem(c + 1, cols)),
            device_id_type=MESH,
        )

    def receiver_arrival(number):
        return pltpu.make_async_remote_copy(
            src_ref=mine,
            dst_ref=receiver_ref.at[number],
            send_sem=out_sem.at[0],
            recv_sem=receiver_sem.at[number],
            device_id=(twin, c),
            device_id_type=MESH,
        )

    def twin_copy(block, number):
        return pltpu.make_async_remote_copy(
            src_ref=block,
            dst_ref=receiver_ref.at[half + number],
            send_sem=twin_sem.at[number],
            recv_sem=receiver_sem.at[half + number],
            device_id=(twin, c),
            device_id_type=MESH,
        )

    @pl.when(on_diagonal)
    def _():
        keep = []
        for step in range(cols):
            number = lax.rem(c + step, cols)
            if step > 0:
                source_arrival(number).wait_recv()
            twin_copy(source_ref.at[number], number).start()
            copy = pltpu.make_async_copy(
                source_ref.at[number], receiver_ref.at[half + number], load_sem.at[step]
            )
            copy.start()
            keep.append(copy)
        for copy in keep:
            copy.wait()

    @pl.when(jnp.logical_not(on_diagonal))
    def _():
        for step in range(cols):
            number = lax.rem(c + step, cols)
            receiver_arrival(half + number).wait_recv()
            twin_copy(receiver_ref.at[half + number], number).start()
        for step in range(1, cols):
            source_arrival(lax.rem(c + step, cols)).wait_recv()

    for number in range(cols):
        receiver_arrival(cols - half + number).wait_recv()
    for step in range(1, cols):
        row_copy(step).wait_send()
        plane_copy(step).wait_send()
    for number in range(cols):
        twin_copy(source_ref.at[number], number).wait_send()


def correlate(scale, source_ref, receiver_ref, out_ref, wide, turned, held, sems):
    frames = LANES
    width = source_ref.shape[1]
    windows = width // frames
    groups = out_ref.shape[0] // LAG_GROUP
    wide[...] = source_ref[...].astype(jnp.float32)
    turned[...] = receiver_ref[...].astype(jnp.float32).T.astype(jnp.bfloat16)
    lane = lax.broadcasted_iota(jnp.int32, (source_ref.shape[0], frames), 1)

    def send(group):
        slot = lax.rem(group, SLOTS)
        return pltpu.make_async_copy(
            held.at[slot], out_ref.at[pl.ds(group * LAG_GROUP, LAG_GROUP)], sems.at[slot]
        )

    def step(group, carry):
        slot = lax.rem(group, SLOTS)

        @pl.when(group >= SLOTS)
        def _():
            send(group - SLOTS).wait()

        for inner in range(LAG_GROUP):
            lag = group * LAG_GROUP + inner - MAXLAG
            from_place = lane - lag
            inside = jnp.logical_and(from_place >= 0, from_place < frames)
            shift = lax.rem(lag + frames, frames)
            moved = [
                jnp.where(
                    inside, pltpu.roll(wide[:, s * frames : (s + 1) * frames], shift, 1), 0.0
                ).astype(jnp.bfloat16)
                for s in range(windows)
            ]
            moved = jnp.concatenate(moved, axis=1)
            product = jnp.dot(moved, turned[...], preferred_element_type=jnp.float32)
            held[slot, inner] = product * scale
        send(group).start()
        return carry

    lax.fori_loop(0, groups, step, 0)
    for group in range(groups - SLOTS, groups):
        send(group).wait()


def body(rows, cols, record, taps, plan, quality):
    slots, chans, length = record.shape
    width = SUB * (length // STRIDE)
    smem = pl.BlockSpec(memory_space=pltpu.SMEM)
    vmem = pl.BlockSpec(memory_space=pltpu.VMEM)
    anywhere = pl.BlockSpec(memory_space=pl.ANY)
    source, receiver = pl.pallas_call(
        functools.partial(whiten_and_send, rows, cols),
        out_shape=(
            jax.ShapeDtypeStruct((cols, chans, width), jnp.bfloat16),
            jax.ShapeDtypeStruct((2 * cols, chans, width), jnp.bfloat16),
        ),
        in_specs=[smem, vmem, vmem, anywhere],
        out_specs=(vmem, vmem),
        scratch_shapes=[
            pltpu.VMEM((slots, chans, length), jnp.bfloat16),
            pltpu.VMEM((PARTS * (length // STRIDE), length), jnp.bfloat16),
            pltpu.SemaphoreType.DMA((max(slots, cols),)),
            pltpu.SemaphoreType.DMA((cols,)),
            pltpu.SemaphoreType.DMA((2 * cols,)),
            pltpu.SemaphoreType.DMA((cols,)),
            pltpu.SemaphoreType.DMA((cols,)),
            pltpu.SemaphoreType.DMA((cols,)),
        ],
        compiler_params=pltpu.CompilerParams(
            collective_id=0, has_side_effects=True, vmem_limit_bytes=32 * 2**20
        ),
        name="whiten_and_send",
    )(plan, taps.reshape(1, TAPS), quality.reshape(1, chans), record)
    sources = cols * chans
    receivers = 2 * cols * chans
    return pl.pallas_call(
        functools.partial(correlate, 1.0 / math.sqrt(width)),
        out_shape=jax.ShapeDtypeStruct((LAGS, sources, receivers), jnp.float32),
        in_specs=[vmem, vmem],
        out_specs=anywhere,
        scratch_shapes=[
            pltpu.VMEM((sources, width), jnp.float32),
            pltpu.VMEM((width, receivers), jnp.bfloat16),
            pltpu.VMEM((SLOTS, LAG_GROUP, sources, receivers), jnp.float32),
            pltpu.SemaphoreType.DMA((SLOTS,)),
        ],
        compiler_params=pltpu.CompilerParams(vmem_limit_bytes=32 * 2**20),
        cost_estimate=pl.CostEstimate(
            flops=2 * LAGS * sources * receivers * width,
            bytes_accessed=4 * LAGS * sources * receivers,
            transcendentals=0,
        ),
        name="correlate",
    )(source.reshape(sources, width), receiver.reshape(receivers, width))


def solution(mesh):
    rows, cols = mesh.shape["row"], mesh.shape["col"]
    in_specs = (P(None, ("row", "col"), None), P(), P(), P(("row", "col")))
    out_specs = P(None, "row", "col")
    return jax.shard_map(
        functools.partial(body, rows, cols),
        mesh=mesh,
        in_specs=in_specs,
        out_specs=out_specs,
        check_vma=False,
    )
```

```python
import functools
import math

import jax
import jax.numpy as jnp
from jax import lax
from jax.experimental import pallas as pl
from jax.experimental.pallas import tpu as pltpu
from jax.sharding import PartitionSpec as P

STRIDE = 20
TAPS = 200
HALFWIN = 32
MAXLAG = 25
SUB = 4
LAGS = 51
LANES = 128
BAND_FRAMES = 32
BAND_STEP = BAND_FRAMES * STRIDE
BAND_WIDTH = 896
PARTS = 3
LAG_GROUP = 3
SLOTS = 3

MESH = pl.DeviceIdType.MESH
NT = (((1,), (1,)), ((), ()))


def split_parts(values, count):
    parts = []
    for _ in range(count):
        part = values.astype(jnp.bfloat16)
        parts.append(part)
        values = values - part.astype(jnp.float32)
    return parts


def filter_band(tap_row):
    base = jnp.broadcast_to(tap_row, (8, TAPS))
    base = jnp.concatenate([base, jnp.zeros((8, BAND_WIDTH - TAPS), jnp.float32)], axis=1)
    place = lax.broadcasted_iota(jnp.int32, (8, BAND_WIDTH), 0)
    groups = []
    for group in range(BAND_FRAMES // 8):
        held = jnp.zeros((8, BAND_WIDTH), jnp.float32)
        for row in range(8):
            shift = (group * 8 + row) * STRIDE
            moved = base if shift == 0 else pltpu.roll(base, shift, 1)
            held = jnp.where(place == row, moved, held)
        groups.append(held)
    return jnp.concatenate(groups, axis=0)


def nearest_first(cols):
    return [sorted(range(cols), key=lambda other: (abs(other - c), other)) for c in range(cols)]


def whiten_and_send(
    rows, cols, plan_hbm, tap_hbm, quality_hbm, record_ref,
    source_ref, receiver_ref,
    raw, table, plan_ref, tap_ref, quality_ref,
    load_sem, source_sem, receiver_sem, out_sem, plane_sem, twin_sem,
):
    r, c = lax.axis_index("row"), lax.axis_index("col")
    parity = lax.rem(r, 2)
    pair = lax.div(r, 2)
    twin = r + 1 - 2 * parity
    on_diagonal = pair == c
    slots, chans, length = raw.shape
    frames = length // STRIDE
    bits = cols.bit_length() - 1

    loads = [
        pltpu.make_async_copy(tap_hbm, tap_ref, load_sem.at[slots]),
        pltpu.make_async_copy(plan_hbm, plan_ref, load_sem.at[slots + 1]),
        pltpu.make_async_copy(quality_hbm, quality_ref, load_sem.at[slots + 2]),
    ] + [pltpu.make_async_copy(record_ref.at[i], raw.at[i], load_sem.at[i]) for i in range(slots)]
    for load in loads:
        load.start()

    def bit(value, k):
        return lax.rem(lax.div(value, 2**k), 2)

    def across(k):
        return r + 2 * 2**k * (1 - 2 * bit(pair, k))

    barrier = pltpu.get_barrier_semaphore()

    def greet(row, col):
        pl.semaphore_signal(barrier, inc=1, device_id=(row, col), device_id_type=MESH)

    for step in range(1, cols):
        greet(r, lax.rem(c + step, cols))
    for k in range(bits):
        greet(across(k), c)
    greet(twin, c)

    table[...] = jnp.zeros_like(table)
    loads[0].wait()
    band = filter_band(tap_ref[...])
    for number, part in enumerate(split_parts(band, PARTS)):
        for block in range(frames // BAND_FRAMES):
            start = block * BAND_STEP
            width = min(BAND_WIDTH, length - start)
            first = number * frames + block * BAND_FRAMES
            table[first : first + BAND_FRAMES, start : start + width] = part[:, :width]

    for load in loads[1:]:
        load.wait()
    picked = jnp.concatenate([raw[plan_ref[s]] for s in range(SUB)], axis=0)
    summed = lax.dot_general(picked, table[...], NT, preferred_element_type=jnp.float32)
    decimated = summed[:, :frames]
    for number in range(1, PARTS):
        decimated = decimated + summed[:, number * frames : (number + 1) * frames]

    near = lax.broadcasted_iota(jnp.int32, (frames, frames), 0)
    near = jnp.abs(near - lax.broadcasted_iota(jnp.int32, (frames, frames), 1)) <= HALFWIN
    near = near.astype(jnp.float32).astype(jnp.bfloat16)
    envelope = jnp.zeros_like(decimated)
    for part in split_parts(jnp.abs(decimated), PARTS):
        envelope = envelope + jnp.dot(part, near, preferred_element_type=jnp.float32)
    envelope = envelope / (2 * HALFWIN + 1)
    square = lax.broadcasted_iota(jnp.int32, (chans, chans), 0) == lax.broadcasted_iota(
        jnp.int32, (chans, chans), 1
    )
    usable = jnp.broadcast_to(quality_ref[...].astype(jnp.float32), (chans, chans))
    usable = jnp.sum(jnp.where(square, usable, 0.0), axis=1, keepdims=True)
    scaled = decimated / (envelope + 1e-05)
    for s in range(SUB):
        window = scaled[s * chans : (s + 1) * chans] * usable
        source_ref[c, :, s * frames : (s + 1) * frames] = window.astype(jnp.bfloat16)

    pl.semaphore_wait(barrier, cols - 1 + bits + 1)

    def remote(src, dst, send_sem, recv_sem, row, col):
        return pltpu.make_async_remote_copy(
            src_ref=src, dst_ref=dst, send_sem=send_sem, recv_sem=recv_sem,
            device_id=(row, col), device_id_type=MESH,
        )

    def along(step):
        target = lax.rem(pair + step, cols)
        copy = remote(
            source_ref.at[c], source_ref.at[c], out_sem.at[step], source_sem.at[c], r, target
        )
        return target != c, copy

    for step in range(cols):
        other, copy = along(step)
        pl.when(other)(copy.start)

    def source_arrival(number):
        return remote(
            source_ref.at[number], source_ref.at[number], out_sem.at[0], source_sem.at[number],
            r, lax.rem(c + 1, cols),
        )

    half = parity * cols

    def receiver_arrival(number):
        return remote(
            receiver_ref.at[number], receiver_ref.at[number], out_sem.at[0],
            receiver_sem.at[number], twin, c,
        )

    def hand_on(block, number, to, send_sem):
        return remote(
            block, receiver_ref.at[half + number], send_sem, receiver_sem.at[half + number], to, c
        )

    order = nearest_first(cols)

    def place(step):
        number = jnp.int32(order[0][step])
        for column in range(1, cols):
            number = jnp.where(c == column, order[column][step], number)
        return number

    differs = [bit(pair, k) != bit(c, k) for k in range(bits)]

    def passes_on(step, k):
        ahead = range(k + 1) if step % 2 == 0 else range(k, bits)
        free = jnp.logical_not(differs[k])
        for other in ahead:
            free = jnp.logical_and(free, jnp.logical_not(differs[other]))
        return free

    def kept(step):
        number = place(step)
        return pltpu.make_async_copy(
            source_ref.at[number], receiver_ref.at[half + number], load_sem.at[step]
        )

    @pl.when(on_diagonal)
    def _():
        for step in range(cols):
            number = place(step)
            if step > 0:
                source_arrival(number).wait_recv()
            for k in range(bits):
                hand_on(source_ref.at[number], number, across(k), plane_sem.at[step, k]).start()
            hand_on(source_ref.at[number], number, twin, twin_sem.at[step]).start()
            kept(step).start()
        for step in range(cols):
            kept(step).wait()

    @pl.when(jnp.logical_not(on_diagonal))
    def _():
        for step in range(cols):
            number = place(step)
            mine = receiver_ref.at[half + number]
            receiver_arrival(half + number).wait_recv()
            for k in range(bits):
                pl.when(passes_on(step, k))(
                    hand_on(mine, number, across(k), plane_sem.at[step, k]).start
                )
            hand_on(mine, number, twin, twin_sem.at[step]).start()
        for step in range(1, cols):
            source_arrival(lax.rem(c + step, cols)).wait_recv()

    for number in range(cols):
        receiver_arrival(cols - half + number).wait_recv()
    for step in range(cols):
        other, copy = along(step)
        pl.when(other)(copy.wait_send)
        block = receiver_ref.at[half + step]
        for k in range(bits):
            sent = jnp.logical_or(on_diagonal, passes_on(step, k))
            pl.when(sent)(hand_on(block, step, across(k), plane_sem.at[step, k]).wait_send)
        hand_on(block, step, twin, twin_sem.at[step]).wait_send()


def correlate(scale, source_ref, receiver_ref, out_ref, wide, turned, held, sems):
    frames = LANES
    width = source_ref.shape[1]
    windows = width // frames
    groups = out_ref.shape[0] // LAG_GROUP
    wide[...] = source_ref[...].astype(jnp.float32)
    turned[...] = receiver_ref[...].astype(jnp.float32).T.astype(jnp.bfloat16)
    lane = lax.broadcasted_iota(jnp.int32, (source_ref.shape[0], frames), 1)

    def send(group):
        slot = lax.rem(group, SLOTS)
        return pltpu.make_async_copy(
            held.at[slot], out_ref.at[pl.ds(group * LAG_GROUP, LAG_GROUP)], sems.at[slot]
        )

    def step(group, carry):
        slot = lax.rem(group, SLOTS)

        @pl.when(group >= SLOTS)
        def _():
            send(group - SLOTS).wait()

        for inner in range(LAG_GROUP):
            lag = group * LAG_GROUP + inner - MAXLAG
            from_place = lane - lag
            inside = jnp.logical_and(from_place >= 0, from_place < frames)
            shift = lax.rem(lag + frames, frames)
            moved = [
                jnp.where(
                    inside, pltpu.roll(wide[:, s * frames : (s + 1) * frames], shift, 1), 0.0
                ).astype(jnp.bfloat16)
                for s in range(windows)
            ]
            moved = jnp.concatenate(moved, axis=1)
            product = jnp.dot(moved, turned[...], preferred_element_type=jnp.float32)
            held[slot, inner] = product * scale
        send(group).start()
        return carry

    lax.fori_loop(0, groups, step, 0)
    for group in range(groups - SLOTS, groups):
        send(group).wait()


def body(rows, cols, record, taps, plan, quality):
    slots, chans, length = record.shape
    width = SUB * (length // STRIDE)
    hbm = pl.BlockSpec(memory_space=pltpu.HBM)
    vmem = pl.BlockSpec(memory_space=pltpu.VMEM)
    anywhere = pl.BlockSpec(memory_space=pl.ANY)
    operands = (plan, taps.reshape(1, TAPS), quality.reshape(1, chans), record)
    source, receiver = pl.pallas_call(
        functools.partial(whiten_and_send, rows, cols),
        out_shape=(
            jax.ShapeDtypeStruct((cols, chans, width), jnp.bfloat16),
            jax.ShapeDtypeStruct((2 * cols, chans, width), jnp.bfloat16),
        ),
        in_specs=[hbm] * 4,
        out_specs=(vmem, vmem),
        scratch_shapes=[
            pltpu.VMEM((slots, chans, length), jnp.bfloat16),
            pltpu.VMEM((PARTS * (length // STRIDE), length), jnp.bfloat16),
            pltpu.SMEM(plan.shape, jnp.int32),
            pltpu.VMEM((1, TAPS), jnp.float32),
            pltpu.VMEM((1, chans), jnp.int32),
            pltpu.SemaphoreType.DMA((max(slots + 3, cols),)),
            pltpu.SemaphoreType.DMA((cols,)),
            pltpu.SemaphoreType.DMA((2 * cols,)),
            pltpu.SemaphoreType.DMA((cols,)),
            pltpu.SemaphoreType.DMA((cols, cols.bit_length() - 1)),
            pltpu.SemaphoreType.DMA((cols,)),
        ],
        compiler_params=pltpu.CompilerParams(
            collective_id=0, has_side_effects=True, vmem_limit_bytes=32 * 2**20
        ),
        name="whiten_and_send",
    )(*(pltpu.with_memory_space_constraint(held, pltpu.HBM) for held in operands))
    sources = cols * chans
    receivers = 2 * cols * chans
    return pl.pallas_call(
        functools.partial(correlate, 1.0 / math.sqrt(width)),
        out_shape=jax.ShapeDtypeStruct((LAGS, sources, receivers), jnp.float32),
        in_specs=[vmem, vmem],
        out_specs=anywhere,
        scratch_shapes=[
            pltpu.VMEM((sources, width), jnp.float32),
            pltpu.VMEM((width, receivers), jnp.bfloat16),
            pltpu.VMEM((SLOTS, LAG_GROUP, sources, receivers), jnp.float32),
            pltpu.SemaphoreType.DMA((SLOTS,)),
        ],
        compiler_params=pltpu.CompilerParams(vmem_limit_bytes=32 * 2**20),
        cost_estimate=pl.CostEstimate(
            flops=2 * LAGS * sources * receivers * width,
            bytes_accessed=4 * LAGS * sources * receivers,
            transcendentals=0,
        ),
        name="correlate",
    )(source.reshape(sources, width), receiver.reshape(receivers, width))


def solution(mesh):
    rows, cols = mesh.shape["row"], mesh.shape["col"]
    in_specs = (P(None, ("row", "col"), None), P(), P(), P(("row", "col")))
    out_specs = P(None, "row", "col")
    return jax.shard_map(
        functools.partial(body, rows, cols),
        mesh=mesh,
        in_specs=in_specs,
        out_specs=out_specs,
        check_vma=False,
    )
```

```python
import functools
import math

import jax
import jax.numpy as jnp
from jax import lax
from jax.experimental import pallas as pl
from jax.experimental.pallas import tpu as pltpu
from jax.sharding import PartitionSpec as P

STRIDE = 20
TAPS = 200
HALFWIN = 32
MAXLAG = 25
SUB = 4
LAGS = 51
LANES = 128
BAND_FRAMES = 32
BAND_STEP = BAND_FRAMES * STRIDE
BAND_WIDTH = 896
PARTS = 3
LAG_GROUP = 3
SLOTS = 3

MESH = pl.DeviceIdType.MESH
NT = (((1,), (1,)), ((), ()))


def split_parts(values, count):
    parts = []
    for _ in range(count):
        part = values.astype(jnp.bfloat16)
        parts.append(part)
        values = values - part.astype(jnp.float32)
    return parts


def filter_band(tap_row):
    base = jnp.broadcast_to(tap_row, (8, TAPS))
    base = jnp.concatenate([base, jnp.zeros((8, BAND_WIDTH - TAPS), jnp.float32)], axis=1)
    place = lax.broadcasted_iota(jnp.int32, (8, BAND_WIDTH), 0)
    groups = []
    for group in range(BAND_FRAMES // 8):
        held = jnp.zeros((8, BAND_WIDTH), jnp.float32)
        for row in range(8):
            shift = (group * 8 + row) * STRIDE
            moved = base if shift == 0 else pltpu.roll(base, shift, 1)
            held = jnp.where(place == row, moved, held)
        groups.append(held)
    return jnp.concatenate(groups, axis=0)


def nearest_first(cols):
    return [sorted(range(cols), key=lambda other: (abs(other - c), other)) for c in range(cols)]


def whiten_and_send(
    rows, cols, plan_hbm, tap_hbm, quality_hbm, record_ref,
    source_ref, receiver_ref,
    raw, table, plan_ref, tap_ref, quality_ref,
    load_sem, source_sem, receiver_sem, out_sem, plane_sem, twin_sem,
):
    r, c = lax.axis_index("row"), lax.axis_index("col")
    parity = lax.rem(r, 2)
    pair = lax.div(r, 2)
    twin = r + 1 - 2 * parity
    on_diagonal = pair == c
    slots, chans, length = raw.shape
    frames = length // STRIDE
    bits = cols.bit_length() - 1

    loads = [
        pltpu.make_async_copy(tap_hbm, tap_ref, load_sem.at[slots]),
        pltpu.make_async_copy(plan_hbm, plan_ref, load_sem.at[slots + 1]),
        pltpu.make_async_copy(quality_hbm, quality_ref, load_sem.at[slots + 2]),
    ] + [pltpu.make_async_copy(record_ref.at[i], raw.at[i], load_sem.at[i]) for i in range(slots)]
    for load in loads:
        load.start()

    def bit(value, k):
        return lax.rem(lax.div(value, 2**k), 2)

    def across(k):
        return r + 2 * 2**k * (1 - 2 * bit(pair, k))

    barrier = pltpu.get_barrier_semaphore()

    def greet(row, col):
        pl.semaphore_signal(barrier, inc=1, device_id=(row, col), device_id_type=MESH)

    for step in range(1, cols):
        greet(r, lax.rem(c + step, cols))
    for k in range(bits):
        greet(across(k), c)
    greet(twin, c)

    table[...] = jnp.zeros_like(table)
    loads[0].wait()
    band = filter_band(tap_ref[...])
    for number, part in enumerate(split_parts(band, PARTS)):
        for block in range(frames // BAND_FRAMES):
            start = block * BAND_STEP
            width = min(BAND_WIDTH, length - start)
            first = number * frames + block * BAND_FRAMES
            table[first : first + BAND_FRAMES, start : start + width] = part[:, :width]

    for load in loads[1:]:
        load.wait()
    picked = jnp.concatenate([raw[plan_ref[s]] for s in range(SUB)], axis=0)
    summed = lax.dot_general(picked, table[...], NT, preferred_element_type=jnp.float32)
    decimated = summed[:, :frames]
    for number in range(1, PARTS):
        decimated = decimated + summed[:, number * frames : (number + 1) * frames]

    near = lax.broadcasted_iota(jnp.int32, (frames, frames), 0)
    near = jnp.abs(near - lax.broadcasted_iota(jnp.int32, (frames, frames), 1)) <= HALFWIN
    near = near.astype(jnp.float32).astype(jnp.bfloat16)
    envelope = jnp.zeros_like(decimated)
    for part in split_parts(jnp.abs(decimated), PARTS):
        envelope = envelope + jnp.dot(part, near, preferred_element_type=jnp.float32)
    envelope = envelope / (2 * HALFWIN + 1)
    square = lax.broadcasted_iota(jnp.int32, (chans, chans), 0) == lax.broadcasted_iota(
        jnp.int32, (chans, chans), 1
    )
    usable = jnp.broadcast_to(quality_ref[...].astype(jnp.float32), (chans, chans))
    usable = jnp.sum(jnp.where(square, usable, 0.0), axis=1, keepdims=True)
    scaled = decimated / (envelope + 1e-05)
    for s in range(SUB):
        window = scaled[s * chans : (s + 1) * chans] * usable
        source_ref[c, :, s * frames : (s + 1) * frames] = window.astype(jnp.bfloat16)

    pl.semaphore_wait(barrier, cols - 1 + bits + 1)

    def remote(src, dst, send_sem, recv_sem, row, col):
        return pltpu.make_async_remote_copy(
            src_ref=src, dst_ref=dst, send_sem=send_sem, recv_sem=recv_sem,
            device_id=(row, col), device_id_type=MESH,
        )

    def along(step):
        target = lax.rem(pair + step, cols)
        copy = remote(
            source_ref.at[c], source_ref.at[c], out_sem.at[step], source_sem.at[c], r, target
        )
        return target != c, copy

    for step in range(cols):
        other, copy = along(step)
        pl.when(other)(copy.start)

    def source_arrival(number):
        return remote(
            source_ref.at[number], source_ref.at[number], out_sem.at[0], source_sem.at[number],
            r, lax.rem(c + 1, cols),
        )

    half = parity * cols

    def receiver_arrival(number):
        return remote(
            receiver_ref.at[number], receiver_ref.at[number], out_sem.at[0],
            receiver_sem.at[number], twin, c,
        )

    def hand_on(block, number, to, send_sem):
        return remote(
            block, receiver_ref.at[half + number], send_sem, receiver_sem.at[half + number], to, c
        )

    order = nearest_first(cols)

    def place(step):
        number = jnp.int32(order[0][step])
        for column in range(1, cols):
            number = jnp.where(c == column, order[column][step], number)
        return number

    differs = [bit(pair, k) != bit(c, k) for k in range(bits)]

    def passes_on(step, k):
        ahead = range(k + 1) if step % 2 == 0 else range(k, bits)
        free = jnp.logical_not(differs[k])
        for other in ahead:
            free = jnp.logical_and(free, jnp.logical_not(differs[other]))
        return free

    def kept(step):
        number = place(step)
        return pltpu.make_async_copy(
            source_ref.at[number], receiver_ref.at[half + number], load_sem.at[step]
        )

    @pl.when(on_diagonal)
    def _():
        for step in range(cols):
            number = place(step)
            if step > 0:
                source_arrival(number).wait_recv()
            for k in range(bits):
                hand_on(source_ref.at[number], number, across(k), plane_sem.at[step, k]).start()
            hand_on(source_ref.at[number], number, twin, twin_sem.at[step]).start()
            kept(step).start()
        for step in range(cols):
            kept(step).wait()

    @pl.when(jnp.logical_not(on_diagonal))
    def _():
        for step in range(cols):
            number = place(step)
            mine = receiver_ref.at[half + number]
            receiver_arrival(half + number).wait_recv()
            for k in range(bits):
                pl.when(passes_on(step, k))(
                    hand_on(mine, number, across(k), plane_sem.at[step, k]).start
                )
            hand_on(mine, number, twin, twin_sem.at[step]).start()
        for step in range(1, cols):
            source_arrival(lax.rem(c + step, cols)).wait_recv()

    for number in range(cols):
        receiver_arrival(cols - half + number).wait_recv()
    for step in range(cols):
        other, copy = along(step)
        pl.when(other)(copy.wait_send)
        block = receiver_ref.at[half + step]
        for k in range(bits):
            sent = jnp.logical_or(on_diagonal, passes_on(step, k))
            pl.when(sent)(hand_on(block, step, across(k), plane_sem.at[step, k]).wait_send)
        hand_on(block, step, twin, twin_sem.at[step]).wait_send()


def correlate(scale, source_ref, receiver_ref, out_ref, wide, turned, even, odd, held, sems):
    frames = LANES
    sources, width = source_ref.shape
    windows = width // frames
    groups = out_ref.shape[0] // LAG_GROUP
    wide[...] = source_ref[...]
    turned[...] = receiver_ref[...].astype(jnp.float32).T.astype(jnp.bfloat16)
    lane = lax.broadcasted_iota(jnp.int32, (sources, frames), 1)

    def send(group):
        slot = lax.rem(group, SLOTS)
        return pltpu.make_async_copy(
            held.at[slot], out_ref.at[pl.ds(group * LAG_GROUP, LAG_GROUP)], sems.at[slot]
        )

    def fill(moved, group, inner):
        lag = group * LAG_GROUP + inner - MAXLAG
        from_place = lane - lag
        inside = jnp.logical_and(from_place >= 0, from_place < frames)
        shift = lax.rem(lag + frames, frames)
        for s in range(windows):
            window = pltpu.roll(wide[:, s * frames : (s + 1) * frames], shift, 1)
            moved[inner * sources : (inner + 1) * sources, s * frames : (s + 1) * frames] = (
                jnp.where(inside, window, 0.0).astype(jnp.bfloat16)
            )

    def multiply(moved, slot, inner):
        product = jnp.dot(
            moved[inner * sources : (inner + 1) * sources, :],
            turned[...],
            preferred_element_type=jnp.float32,
        )
        held[slot, inner] = product * scale

    def turn(group, now, later):
        slot = lax.rem(group, SLOTS)

        @pl.when(group >= SLOTS)
        def _():
            send(group - SLOTS).wait()

        for inner in range(LAG_GROUP):
            multiply(now, slot, inner)
            if later is not None:
                fill(later, group + 1, inner)
        send(group).start()

    for inner in range(LAG_GROUP):
        fill(even, 0, inner)

    def step(index, carry):
        turn(2 * index, even, odd)
        turn(2 * index + 1, odd, even)
        return carry

    lax.fori_loop(0, groups // 2, step, 0)
    turn(groups - 1, even, None)
    for group in range(groups - SLOTS, groups):
        send(group).wait()


def body(rows, cols, record, taps, plan, quality):
    slots, chans, length = record.shape
    width = SUB * (length // STRIDE)
    hbm = pl.BlockSpec(memory_space=pltpu.HBM)
    vmem = pl.BlockSpec(memory_space=pltpu.VMEM)
    anywhere = pl.BlockSpec(memory_space=pl.ANY)
    operands = (plan, taps.reshape(1, TAPS), quality.reshape(1, chans), record)
    source, receiver = pl.pallas_call(
        functools.partial(whiten_and_send, rows, cols),
        out_shape=(
            jax.ShapeDtypeStruct((cols, chans, width), jnp.bfloat16),
            jax.ShapeDtypeStruct((2 * cols, chans, width), jnp.bfloat16),
        ),
        in_specs=[hbm] * 4,
        out_specs=(vmem, vmem),
        scratch_shapes=[
            pltpu.VMEM((slots, chans, length), jnp.bfloat16),
            pltpu.VMEM((PARTS * (length // STRIDE), length), jnp.bfloat16),
            pltpu.SMEM(plan.shape, jnp.int32),
            pltpu.VMEM((1, TAPS), jnp.float32),
            pltpu.VMEM((1, chans), jnp.int32),
            pltpu.SemaphoreType.DMA((max(slots + 3, cols),)),
            pltpu.SemaphoreType.DMA((cols,)),
            pltpu.SemaphoreType.DMA((2 * cols,)),
            pltpu.SemaphoreType.DMA((cols,)),
            pltpu.SemaphoreType.DMA((cols, cols.bit_length() - 1)),
            pltpu.SemaphoreType.DMA((cols,)),
        ],
        compiler_params=pltpu.CompilerParams(
            collective_id=0, has_side_effects=True, vmem_limit_bytes=32 * 2**20
        ),
        name="whiten_and_send",
    )(*(pltpu.with_memory_space_constraint(held, pltpu.HBM) for held in operands))
    sources = cols * chans
    receivers = 2 * cols * chans
    return pl.pallas_call(
        functools.partial(correlate, 1.0 / math.sqrt(width)),
        out_shape=jax.ShapeDtypeStruct((LAGS, sources, receivers), jnp.float32),
        in_specs=[vmem, vmem],
        out_specs=anywhere,
        scratch_shapes=[
            pltpu.VMEM((sources, width), jnp.bfloat16),
            pltpu.VMEM((width, receivers), jnp.bfloat16),
            pltpu.VMEM((LAG_GROUP * sources, width), jnp.bfloat16),
            pltpu.VMEM((LAG_GROUP * sources, width), jnp.bfloat16),
            pltpu.VMEM((SLOTS, LAG_GROUP, sources, receivers), jnp.float32),
            pltpu.SemaphoreType.DMA((SLOTS,)),
        ],
        compiler_params=pltpu.CompilerParams(vmem_limit_bytes=32 * 2**20),
        cost_estimate=pl.CostEstimate(
            flops=2 * LAGS * sources * receivers * width,
            bytes_accessed=4 * LAGS * sources * receivers,
            transcendentals=0,
        ),
        name="correlate",
    )(source.reshape(sources, width), receiver.reshape(receivers, width))


def solution(mesh):
    rows, cols = mesh.shape["row"], mesh.shape["col"]
    in_specs = (P(None, ("row", "col"), None), P(), P(), P(("row", "col")))
    out_specs = P(None, "row", "col")
    return jax.shard_map(
        functools.partial(body, rows, cols),
        mesh=mesh,
        in_specs=in_specs,
        out_specs=out_specs,
        check_vma=False,
    )
```

```python
import functools
import math

import jax
import jax.numpy as jnp
from jax import lax
from jax.experimental import pallas as pl
from jax.experimental.pallas import tpu as pltpu
from jax.sharding import PartitionSpec as P

STRIDE = 20
TAPS = 200
HALFWIN = 32
MAXLAG = 25
SUB = 4
LAGS = 51
LANES = 128
BAND_FRAMES = 32
BAND_STEP = BAND_FRAMES * STRIDE
BAND_WIDTH = 896
PARTS = 3
LAG_GROUP = 3
SLOTS = 3
CHUNKS = 2

MESH = pl.DeviceIdType.MESH
NT = (((1,), (1,)), ((), ()))


def split_parts(values, count):
    parts = []
    for _ in range(count):
        part = values.astype(jnp.bfloat16)
        parts.append(part)
        values = values - part.astype(jnp.float32)
    return parts


def filter_band(tap_row):
    base = jnp.broadcast_to(tap_row, (8, TAPS))
    base = jnp.concatenate([base, jnp.zeros((8, BAND_WIDTH - TAPS), jnp.float32)], axis=1)
    place = lax.broadcasted_iota(jnp.int32, (8, BAND_WIDTH), 0)
    groups = []
    for group in range(BAND_FRAMES // 8):
        held = jnp.zeros((8, BAND_WIDTH), jnp.float32)
        for row in range(8):
            shift = (group * 8 + row) * STRIDE
            moved = base if shift == 0 else pltpu.roll(base, shift, 1)
            held = jnp.where(place == row, moved, held)
        groups.append(held)
    return jnp.concatenate(groups, axis=0)


def nearest_first(cols):
    return [sorted(range(cols), key=lambda other: (abs(other - c), other)) for c in range(cols)]


def whiten_and_send(
    rows, cols, plan_hbm, tap_hbm, quality_hbm, record_ref,
    source_ref, turned_ref,
    receiver_ref, raw, table, plan_ref, tap_ref, quality_ref,
    load_sem, keep_sem, source_sem, receiver_sem, out_sem, plane_sem, twin_sem,
):
    r, c = lax.axis_index("row"), lax.axis_index("col")
    parity = lax.rem(r, 2)
    pair = lax.div(r, 2)
    twin = r + 1 - 2 * parity
    on_diagonal = pair == c
    slots, chans, length = raw.shape
    frames = length // STRIDE
    bits = cols.bit_length() - 1

    loads = [
        pltpu.make_async_copy(tap_hbm, tap_ref, load_sem.at[slots]),
        pltpu.make_async_copy(plan_hbm, plan_ref, load_sem.at[slots + 1]),
        pltpu.make_async_copy(quality_hbm, quality_ref, load_sem.at[slots + 2]),
    ] + [pltpu.make_async_copy(record_ref.at[i], raw.at[i], load_sem.at[i]) for i in range(slots)]
    for load in loads:
        load.start()

    def bit(value, k):
        return lax.rem(lax.div(value, 2**k), 2)

    def across(k):
        return r + 2 * 2**k * (1 - 2 * bit(pair, k))

    barrier = pltpu.get_barrier_semaphore()

    def greet(row, col):
        pl.semaphore_signal(barrier, inc=1, device_id=(row, col), device_id_type=MESH)

    for step in range(1, cols):
        greet(r, lax.rem(c + step, cols))
    for k in range(bits):
        greet(across(k), c)
    greet(twin, c)

    table[...] = jnp.zeros_like(table)
    loads[0].wait()
    band = filter_band(tap_ref[...])
    for number, part in enumerate(split_parts(band, PARTS)):
        for block in range(frames // BAND_FRAMES):
            start = block * BAND_STEP
            width = min(BAND_WIDTH, length - start)
            first = number * frames + block * BAND_FRAMES
            table[first : first + BAND_FRAMES, start : start + width] = part[:, :width]

    for load in loads[1:]:
        load.wait()
    picked = jnp.concatenate([raw[plan_ref[s]] for s in range(SUB)], axis=0)
    summed = lax.dot_general(picked, table[...], NT, preferred_element_type=jnp.float32)
    decimated = summed[:, :frames]
    for number in range(1, PARTS):
        decimated = decimated + summed[:, number * frames : (number + 1) * frames]

    near = lax.broadcasted_iota(jnp.int32, (frames, frames), 0)
    near = jnp.abs(near - lax.broadcasted_iota(jnp.int32, (frames, frames), 1)) <= HALFWIN
    near = near.astype(jnp.float32).astype(jnp.bfloat16)
    square = lax.broadcasted_iota(jnp.int32, (chans, chans), 0) == lax.broadcasted_iota(
        jnp.int32, (chans, chans), 1
    )
    usable = jnp.broadcast_to(quality_ref[...].astype(jnp.float32), (chans, chans))
    usable = jnp.sum(jnp.where(square, usable, 0.0), axis=1, keepdims=True)
    windows = SUB // CHUNKS

    def whiten(chunk):
        part = decimated[chunk * windows * chans : (chunk + 1) * windows * chans]
        envelope = jnp.zeros_like(part)
        for piece in split_parts(jnp.abs(part), PARTS):
            envelope = envelope + jnp.dot(piece, near, preferred_element_type=jnp.float32)
        scaled = part / (envelope / (2 * HALFWIN + 1) + 1e-05)
        for s in range(windows):
            window = scaled[s * chans : (s + 1) * chans] * usable
            source_ref[chunk, c, :, s * frames : (s + 1) * frames] = window.astype(jnp.bfloat16)

    def remote(src, dst, send_sem, recv_sem, row, col):
        return pltpu.make_async_remote_copy(
            src_ref=src, dst_ref=dst, send_sem=send_sem, recv_sem=recv_sem,
            device_id=(row, col), device_id_type=MESH,
        )

    def along(chunk, step):
        target = lax.rem(pair + step, cols)
        mine = source_ref.at[chunk, c]
        copy = remote(mine, mine, out_sem.at[chunk, step], source_sem.at[chunk, c], r, target)
        return target != c, copy

    def source_arrival(chunk, number):
        block = source_ref.at[chunk, number]
        return remote(
            block, block, out_sem.at[0, 0], source_sem.at[chunk, number],
            r, lax.rem(c + 1, cols),
        )

    half = parity * cols

    def receiver_arrival(chunk, number):
        block = receiver_ref.at[chunk, number]
        return remote(
            block, block, out_sem.at[0, 0], receiver_sem.at[chunk, number], twin, c
        )

    def hand_on(block, chunk, number, to, send_sem):
        return remote(
            block, receiver_ref.at[chunk, half + number], send_sem,
            receiver_sem.at[chunk, half + number], to, c,
        )

    for chunk in range(CHUNKS):
        whiten(chunk)
        if chunk == 0:
            pl.semaphore_wait(barrier, cols - 1 + bits + 1)
        other, copy = along(chunk, 0)
        pl.when(other)(copy.start)
    for chunk in range(CHUNKS):
        for step in range(1, cols):
            other, copy = along(chunk, step)
            pl.when(other)(copy.start)

    order = nearest_first(cols)

    def place(step):
        number = jnp.int32(order[0][step])
        for column in range(1, cols):
            number = jnp.where(c == column, order[column][step], number)
        return number

    differs = [bit(pair, k) != bit(c, k) for k in range(bits)]

    def passes_on(step, k):
        ahead = range(k + 1) if step % 2 == 0 else range(k, bits)
        free = jnp.logical_not(differs[k])
        for other in ahead:
            free = jnp.logical_and(free, jnp.logical_not(differs[other]))
        return free

    def kept(chunk, step):
        number = place(step)
        return pltpu.make_async_copy(
            source_ref.at[chunk, number],
            receiver_ref.at[chunk, half + number],
            keep_sem.at[chunk, step],
        )

    every = [(chunk, step) for chunk in range(CHUNKS) for step in range(cols)]

    @pl.when(on_diagonal)
    def _():
        for chunk, step in every:
            number = place(step)
            if step > 0:
                source_arrival(chunk, number).wait_recv()
            mine = source_ref.at[chunk, number]
            for k in range(bits):
                hand_on(mine, chunk, number, across(k), plane_sem.at[chunk, step, k]).start()
            hand_on(mine, chunk, number, twin, twin_sem.at[chunk, step]).start()
            kept(chunk, step).start()
        for chunk, step in every:
            kept(chunk, step).wait()

    @pl.when(jnp.logical_not(on_diagonal))
    def _():
        for chunk, step in every:
            number = place(step)
            mine = receiver_ref.at[chunk, half + number]
            receiver_arrival(chunk, half + number).wait_recv()
            for k in range(bits):
                pl.when(passes_on(step, k))(
                    hand_on(mine, chunk, number, across(k), plane_sem.at[chunk, step, k]).start
                )
            hand_on(mine, chunk, number, twin, twin_sem.at[chunk, step]).start()
        for chunk, step in every:
            if step > 0:
                source_arrival(chunk, lax.rem(c + step, cols)).wait_recv()

    width = windows * frames
    for chunk in range(CHUNKS):
        for number in range(cols):
            receiver_arrival(chunk, cols - half + number).wait_recv()
        whole = receiver_ref[chunk].reshape(2 * cols * chans, width)
        turned_ref[chunk * width : (chunk + 1) * width, :] = (
            whole.astype(jnp.float32).T.astype(jnp.bfloat16)
        )
    for chunk, step in every:
        other, copy = along(chunk, step)
        pl.when(other)(copy.wait_send)
        block = receiver_ref.at[chunk, half + step]
        for k in range(bits):
            sent = jnp.logical_or(on_diagonal, passes_on(step, k))
            pl.when(sent)(
                hand_on(block, chunk, step, across(k), plane_sem.at[chunk, step, k]).wait_send
            )
        hand_on(block, chunk, step, twin, twin_sem.at[chunk, step]).wait_send()


def correlate(scale, source_ref, turned, out_ref, even, odd, held, sems):
    frames = LANES
    chunks, sources, width = source_ref.shape
    windows = width // frames
    groups = out_ref.shape[0] // LAG_GROUP
    lane = lax.broadcasted_iota(jnp.int32, (sources, frames), 1)

    def send(group):
        slot = lax.rem(group, SLOTS)
        return pltpu.make_async_copy(
            held.at[slot], out_ref.at[pl.ds(group * LAG_GROUP, LAG_GROUP)], sems.at[slot]
        )

    def fill(moved, group, inner):
        lag = group * LAG_GROUP + inner - MAXLAG
        from_place = lane - lag
        inside = jnp.logical_and(from_place >= 0, from_place < frames)
        shift = lax.rem(lag + frames, frames)
        rows = slice(inner * sources, (inner + 1) * sources)
        for s in range(chunks * windows):
            place = s % windows * frames
            window = pltpu.roll(source_ref[s // windows, :, place : place + frames], shift, 1)
            moved[rows, s * frames : (s + 1) * frames] = jnp.where(inside, window, 0.0).astype(
                jnp.bfloat16
            )

    def multiply(moved, slot, inner):
        product = jnp.dot(
            moved[inner * sources : (inner + 1) * sources, :],
            turned[...],
            preferred_element_type=jnp.float32,
        )
        held[slot, inner] = product * scale

    def turn(group, now, later):
        slot = lax.rem(group, SLOTS)

        @pl.when(group >= SLOTS)
        def _():
            send(group - SLOTS).wait()

        for inner in range(LAG_GROUP):
            multiply(now, slot, inner)
            fill(later, group + 1, inner)
        send(group).start()

    for inner in range(LAG_GROUP):
        fill(even, 0, inner)
        multiply(even, 0, inner)
        pltpu.make_async_copy(held.at[0, inner], out_ref.at[inner], sems.at[0]).start()
    for inner in range(LAG_GROUP):
        fill(odd, 1, inner)

    def step(index, carry):
        turn(2 * index + 1, odd, even)
        turn(2 * index + 2, even, odd)
        return carry

    lax.fori_loop(0, groups // 2, step, 0)
    for group in range(groups - SLOTS, groups):
        send(group).wait()


def body(rows, cols, record, taps, plan, quality):
    slots, chans, length = record.shape
    width = SUB * (length // STRIDE)
    hbm = pl.BlockSpec(memory_space=pltpu.HBM)
    vmem = pl.BlockSpec(memory_space=pltpu.VMEM)
    anywhere = pl.BlockSpec(memory_space=pl.ANY)
    operands = (plan, taps.reshape(1, TAPS), quality.reshape(1, chans), record)
    sources = cols * chans
    receivers = 2 * sources
    bits = cols.bit_length() - 1
    source, turned = pl.pallas_call(
        functools.partial(whiten_and_send, rows, cols),
        out_shape=(
            jax.ShapeDtypeStruct((CHUNKS, cols, chans, width // CHUNKS), jnp.bfloat16),
            jax.ShapeDtypeStruct((width, receivers), jnp.bfloat16),
        ),
        in_specs=[hbm] * 4,
        out_specs=(vmem, vmem),
        scratch_shapes=[
            pltpu.VMEM((CHUNKS, 2 * cols, chans, width // CHUNKS), jnp.bfloat16),
            pltpu.VMEM((slots, chans, length), jnp.bfloat16),
            pltpu.VMEM((PARTS * (length // STRIDE), length), jnp.bfloat16),
            pltpu.SMEM(plan.shape, jnp.int32),
            pltpu.VMEM((1, TAPS), jnp.float32),
            pltpu.VMEM((1, chans), jnp.int32),
            pltpu.SemaphoreType.DMA((slots + 3,)),
            pltpu.SemaphoreType.DMA((CHUNKS, cols)),
            pltpu.SemaphoreType.DMA((CHUNKS, cols)),
            pltpu.SemaphoreType.DMA((CHUNKS, 2 * cols)),
            pltpu.SemaphoreType.DMA((CHUNKS, cols)),
            pltpu.SemaphoreType.DMA((CHUNKS, cols, bits)),
            pltpu.SemaphoreType.DMA((CHUNKS, cols)),
        ],
        compiler_params=pltpu.CompilerParams(
            collective_id=0, has_side_effects=True, vmem_limit_bytes=32 * 2**20
        ),
        name="whiten_and_send",
    )(*(pltpu.with_memory_space_constraint(held, pltpu.HBM) for held in operands))
    return pl.pallas_call(
        functools.partial(correlate, 1.0 / math.sqrt(width)),
        out_shape=jax.ShapeDtypeStruct((LAGS, sources, receivers), jnp.float32),
        in_specs=[vmem, vmem],
        out_specs=anywhere,
        scratch_shapes=[
            pltpu.VMEM((LAG_GROUP * sources, width), jnp.bfloat16),
            pltpu.VMEM((LAG_GROUP * sources, width), jnp.bfloat16),
            pltpu.VMEM((SLOTS, LAG_GROUP, sources, receivers), jnp.float32),
            pltpu.SemaphoreType.DMA((SLOTS,)),
        ],
        compiler_params=pltpu.CompilerParams(vmem_limit_bytes=32 * 2**20),
        cost_estimate=pl.CostEstimate(
            flops=2 * LAGS * sources * receivers * width,
            bytes_accessed=4 * LAGS * sources * receivers,
            transcendentals=0,
        ),
        name="correlate",
    )(source.reshape(CHUNKS, sources, width // CHUNKS), turned)


def solution(mesh):
    rows, cols = mesh.shape["row"], mesh.shape["col"]
    in_specs = (P(None, ("row", "col"), None), P(), P(), P(("row", "col")))
    out_specs = P(None, "row", "col")
    return jax.shard_map(
        functools.partial(body, rows, cols),
        mesh=mesh,
        in_specs=in_specs,
        out_specs=out_specs,
        check_vma=False,
    )
```

```python
import functools
import math

import jax
import jax.numpy as jnp
from jax import lax
from jax.experimental import pallas as pl
from jax.experimental.pallas import tpu as pltpu
from jax.sharding import PartitionSpec as P

STRIDE = 20
TAPS = 200
HALFWIN = 32
MAXLAG = 25
SUB = 4
LAGS = 51
LANES = 128
BAND_FRAMES = 32
BAND_STEP = BAND_FRAMES * STRIDE
BAND_WIDTH = 896
PARTS = 3
LAG_GROUP = 3
SLOTS = 3
CHUNKS = 2

MESH = pl.DeviceIdType.MESH
NT = (((1,), (1,)), ((), ()))


def split_parts(values, count):
    parts = []
    for _ in range(count):
        part = values.astype(jnp.bfloat16)
        parts.append(part)
        values = values - part.astype(jnp.float32)
    return parts


def filter_band(tap_row):
    base = jnp.broadcast_to(tap_row, (8, TAPS))
    base = jnp.concatenate([base, jnp.zeros((8, BAND_WIDTH - TAPS), jnp.float32)], axis=1)
    place = lax.broadcasted_iota(jnp.int32, (8, BAND_WIDTH), 0)
    groups = []
    for group in range(BAND_FRAMES // 8):
        held = jnp.zeros((8, BAND_WIDTH), jnp.float32)
        for row in range(8):
            shift = (group * 8 + row) * STRIDE
            moved = base if shift == 0 else pltpu.roll(base, shift, 1)
            held = jnp.where(place == row, moved, held)
        groups.append(held)
    return jnp.concatenate(groups, axis=0)


def nearest_first(cols):
    return [sorted(range(cols), key=lambda other: (abs(other - c), other)) for c in range(cols)]


def whiten_and_send(
    rows, cols, plan_hbm, tap_hbm, quality_hbm, record_ref,
    source_ref, turned_ref,
    receiver_ref, raw, table, plan_ref, tap_ref, quality_ref,
    load_sem, keep_sem, source_sem, receiver_sem, out_sem, plane_sem, twin_sem,
):
    r, c = lax.axis_index("row"), lax.axis_index("col")
    parity = lax.rem(r, 2)
    pair = lax.div(r, 2)
    twin = r + 1 - 2 * parity
    on_diagonal = pair == c
    slots, chans, length = raw.shape
    frames = length // STRIDE
    bits = cols.bit_length() - 1

    loads = [
        pltpu.make_async_copy(tap_hbm, tap_ref, load_sem.at[slots]),
        pltpu.make_async_copy(plan_hbm, plan_ref, load_sem.at[slots + 1]),
        pltpu.make_async_copy(quality_hbm, quality_ref, load_sem.at[slots + 2]),
    ] + [pltpu.make_async_copy(record_ref.at[i], raw.at[i], load_sem.at[i]) for i in range(slots)]
    for load in loads:
        load.start()

    def bit(value, k):
        return lax.rem(lax.div(value, 2**k), 2)

    def across(k):
        return r + 2 * 2**k * (1 - 2 * bit(pair, k))

    def other_core(row):
        return row + 1 - 2 * parity

    barrier = pltpu.get_barrier_semaphore()

    def greet(row, col):
        pl.semaphore_signal(barrier, inc=1, device_id=(row, col), device_id_type=MESH)

    for step in range(1, cols):
        greet(r, lax.rem(c + step, cols))
    for k in range(bits):
        greet(across(k), c)
        greet(other_core(across(k)), c)
    greet(twin, c)

    table[...] = jnp.zeros_like(table)
    loads[0].wait()
    band = filter_band(tap_ref[...])
    for number, part in enumerate(split_parts(band, PARTS)):
        for block in range(frames // BAND_FRAMES):
            start = block * BAND_STEP
            width = min(BAND_WIDTH, length - start)
            first = number * frames + block * BAND_FRAMES
            table[first : first + BAND_FRAMES, start : start + width] = part[:, :width]

    for load in loads[1:]:
        load.wait()
    picked = jnp.concatenate([raw[plan_ref[s]] for s in range(SUB)], axis=0)
    summed = lax.dot_general(table[...], picked, NT, preferred_element_type=jnp.float32)
    decimated = summed[:frames]
    for number in range(1, PARTS):
        decimated = decimated + summed[number * frames : (number + 1) * frames]

    near = lax.broadcasted_iota(jnp.int32, (frames, frames), 0)
    near = jnp.abs(near - lax.broadcasted_iota(jnp.int32, (frames, frames), 1)) <= HALFWIN
    near = near.astype(jnp.float32).astype(jnp.bfloat16)
    windows = SUB // CHUNKS
    usable = jnp.concatenate([quality_ref[...].astype(jnp.float32)] * windows, axis=1)

    def whiten(chunk):
        part = decimated[:, chunk * windows * chans : (chunk + 1) * windows * chans]
        envelope = jnp.zeros_like(part)
        for piece in split_parts(jnp.abs(part), PARTS):
            envelope = envelope + jnp.dot(near, piece, preferred_element_type=jnp.float32)
        scaled = (part / (envelope / (2 * HALFWIN + 1) + 1e-05) * usable).T
        for s in range(windows):
            window = scaled[s * chans : (s + 1) * chans]
            source_ref[chunk, c, :, s * frames : (s + 1) * frames] = window.astype(jnp.bfloat16)

    def remote(src, dst, send_sem, recv_sem, row, col):
        return pltpu.make_async_remote_copy(
            src_ref=src, dst_ref=dst, send_sem=send_sem, recv_sem=recv_sem,
            device_id=(row, col), device_id_type=MESH,
        )

    def along(chunk, step):
        target = lax.rem(pair + step, cols)
        mine = source_ref.at[chunk, c]
        copy = remote(mine, mine, out_sem.at[chunk, step], source_sem.at[chunk, c], r, target)
        return target != c, copy

    def source_arrival(chunk, number):
        block = source_ref.at[chunk, number]
        return remote(
            block, block, out_sem.at[0, 0], source_sem.at[chunk, number],
            r, lax.rem(c + 1, cols),
        )

    half = parity * cols

    def receiver_arrival(chunk, number):
        block = receiver_ref.at[chunk, number]
        return remote(
            block, block, out_sem.at[0, 0], receiver_sem.at[chunk, number], twin, c
        )

    def hand_on(block, chunk, number, to, send_sem):
        return remote(
            block, receiver_ref.at[chunk, half + number], send_sem,
            receiver_sem.at[chunk, half + number], to, c,
        )

    for chunk in range(CHUNKS):
        whiten(chunk)
        if chunk == 0:
            pl.semaphore_wait(barrier, cols - 1 + 2 * bits + 1)
        other, copy = along(chunk, 0)
        pl.when(other)(copy.start)
    for chunk in range(CHUNKS):
        for step in range(1, cols):
            other, copy = along(chunk, step)
            pl.when(other)(copy.start)

    order = nearest_first(cols)

    def place(step):
        number = jnp.int32(order[0][step])
        for column in range(1, cols):
            number = jnp.where(c == column, order[column][step], number)
        return number

    differs = [bit(pair, k) != bit(c, k) for k in range(bits)]
    far = sum(jnp.where(differ, 1, 0) for differ in differs) > 1

    def passes_on(step, k):
        ahead = range(k + 1) if step % 2 == 0 else range(k, bits)
        free = jnp.logical_not(differs[k])
        for other in ahead:
            free = jnp.logical_and(free, jnp.logical_not(differs[other]))
        return free

    def kept(chunk, step):
        number = place(step)
        return pltpu.make_async_copy(
            source_ref.at[chunk, number],
            receiver_ref.at[chunk, half + number],
            keep_sem.at[chunk, step],
        )

    every = [(chunk, step) for chunk in range(CHUNKS) for step in range(cols)]

    @pl.when(on_diagonal)
    def _():
        for chunk, step in every:
            number = place(step)
            if step > 0:
                source_arrival(chunk, number).wait_recv()
            mine = source_ref.at[chunk, number]
            for k in range(bits):
                hand_on(mine, chunk, number, across(k), plane_sem.at[chunk, step, k, 0]).start()
            hand_on(mine, chunk, number, twin, twin_sem.at[chunk, step]).start()
            kept(chunk, step).start()
        for chunk, step in every:
            kept(chunk, step).wait()

    @pl.when(jnp.logical_not(on_diagonal))
    def _():
        for chunk, step in every:
            number = place(step)
            mine = receiver_ref.at[chunk, half + number]
            receiver_arrival(chunk, half + number).wait_recv()
            for k in range(bits):
                sends = passes_on(step, k)
                for core, to in enumerate((across(k), other_core(across(k)))):
                    pl.when(sends)(
                        hand_on(mine, chunk, number, to, plane_sem.at[chunk, step, k, core]).start
                    )
            pl.when(jnp.logical_not(far))(
                hand_on(mine, chunk, number, twin, twin_sem.at[chunk, step]).start
            )
        for chunk, step in every:
            if step > 0:
                source_arrival(chunk, lax.rem(c + step, cols)).wait_recv()

    width = windows * frames
    for chunk in range(CHUNKS):
        for number in range(cols):
            receiver_arrival(chunk, cols - half + number).wait_recv()
        whole = receiver_ref[chunk].reshape(2 * cols * chans, width)
        turned_ref[chunk * width : (chunk + 1) * width, :] = (
            whole.astype(jnp.float32).T.astype(jnp.bfloat16)
        )
    for chunk, step in every:
        other, copy = along(chunk, step)
        pl.when(other)(copy.wait_send)
        block = receiver_ref.at[chunk, half + step]
        for k in range(bits):
            sends = passes_on(step, k)
            pl.when(jnp.logical_or(on_diagonal, sends))(
                hand_on(block, chunk, step, across(k), plane_sem.at[chunk, step, k, 0]).wait_send
            )
            pl.when(jnp.logical_and(jnp.logical_not(on_diagonal), sends))(
                hand_on(block, chunk, step, across(k), plane_sem.at[chunk, step, k, 1]).wait_send
            )
        pl.when(jnp.logical_not(far))(
            hand_on(block, chunk, step, twin, twin_sem.at[chunk, step]).wait_send
        )


def correlate(scale, source_ref, turned, out_ref, even, odd, held, sems):
    frames = LANES
    chunks, sources, width = source_ref.shape
    windows = width // frames
    groups = out_ref.shape[0] // LAG_GROUP
    lane = lax.broadcasted_iota(jnp.int32, (sources, frames), 1)

    def send(group):
        slot = lax.rem(group, SLOTS)
        return pltpu.make_async_copy(
            held.at[slot], out_ref.at[pl.ds(group * LAG_GROUP, LAG_GROUP)], sems.at[slot]
        )

    def fill(moved, group, inner):
        lag = group * LAG_GROUP + inner - MAXLAG
        from_place = lane - lag
        inside = jnp.logical_and(from_place >= 0, from_place < frames)
        shift = lax.rem(lag + frames, frames)
        rows = slice(inner * sources, (inner + 1) * sources)
        for s in range(chunks * windows):
            place = s % windows * frames
            window = pltpu.roll(source_ref[s // windows, :, place : place + frames], shift, 1)
            moved[rows, s * frames : (s + 1) * frames] = jnp.where(inside, window, 0.0).astype(
                jnp.bfloat16
            )

    def multiply(rows):
        return jnp.dot(rows, turned[...], preferred_element_type=jnp.float32) * scale

    def turn(group, now, later):
        slot = lax.rem(group, SLOTS)

        @pl.when(group >= SLOTS)
        def _():
            send(group - SLOTS).wait()

        held[slot] = multiply(now[...]).reshape(held.shape[1:])
        for inner in range(LAG_GROUP):
            fill(later, group + 1, inner)
        send(group).start()

    for inner in range(LAG_GROUP):
        fill(even, 0, inner)
        held[0, inner] = multiply(even[inner * sources : (inner + 1) * sources, :])
        pltpu.make_async_copy(held.at[0, inner], out_ref.at[inner], sems.at[0]).start()
    for inner in range(LAG_GROUP):
        fill(odd, 1, inner)

    def step(index, carry):
        turn(2 * index + 1, odd, even)
        turn(2 * index + 2, even, odd)
        return carry

    lax.fori_loop(0, groups // 2, step, 0)
    for group in range(groups - SLOTS, groups):
        send(group).wait()


def body(rows, cols, record, taps, plan, quality):
    slots, chans, length = record.shape
    width = SUB * (length // STRIDE)
    hbm = pl.BlockSpec(memory_space=pltpu.HBM)
    vmem = pl.BlockSpec(memory_space=pltpu.VMEM)
    anywhere = pl.BlockSpec(memory_space=pl.ANY)
    operands = (plan, taps.reshape(1, TAPS), quality.reshape(1, chans), record)
    sources = cols * chans
    receivers = 2 * sources
    bits = cols.bit_length() - 1
    source, turned = pl.pallas_call(
        functools.partial(whiten_and_send, rows, cols),
        out_shape=(
            jax.ShapeDtypeStruct((CHUNKS, cols, chans, width // CHUNKS), jnp.bfloat16),
            jax.ShapeDtypeStruct((width, receivers), jnp.bfloat16),
        ),
        in_specs=[hbm] * 4,
        out_specs=(vmem, vmem),
        scratch_shapes=[
            pltpu.VMEM((CHUNKS, 2 * cols, chans, width // CHUNKS), jnp.bfloat16),
            pltpu.VMEM((slots, chans, length), jnp.bfloat16),
            pltpu.VMEM((PARTS * (length // STRIDE), length), jnp.bfloat16),
            pltpu.SMEM(plan.shape, jnp.int32),
            pltpu.VMEM((1, TAPS), jnp.float32),
            pltpu.VMEM((1, chans), jnp.int32),
            pltpu.SemaphoreType.DMA((slots + 3,)),
            pltpu.SemaphoreType.DMA((CHUNKS, cols)),
            pltpu.SemaphoreType.DMA((CHUNKS, cols)),
            pltpu.SemaphoreType.DMA((CHUNKS, 2 * cols)),
            pltpu.SemaphoreType.DMA((CHUNKS, cols)),
            pltpu.SemaphoreType.DMA((CHUNKS, cols, bits, 2)),
            pltpu.SemaphoreType.DMA((CHUNKS, cols)),
        ],
        compiler_params=pltpu.CompilerParams(
            collective_id=0, has_side_effects=True, vmem_limit_bytes=32 * 2**20
        ),
        name="whiten_and_send",
    )(*(pltpu.with_memory_space_constraint(held, pltpu.HBM) for held in operands))
    return pl.pallas_call(
        functools.partial(correlate, 1.0 / math.sqrt(width)),
        out_shape=jax.ShapeDtypeStruct((LAGS, sources, receivers), jnp.float32),
        in_specs=[vmem, vmem],
        out_specs=anywhere,
        scratch_shapes=[
            pltpu.VMEM((LAG_GROUP * sources, width), jnp.bfloat16),
            pltpu.VMEM((LAG_GROUP * sources, width), jnp.bfloat16),
            pltpu.VMEM((SLOTS, LAG_GROUP, sources, receivers), jnp.float32),
            pltpu.SemaphoreType.DMA((SLOTS,)),
        ],
        compiler_params=pltpu.CompilerParams(vmem_limit_bytes=32 * 2**20),
        cost_estimate=pl.CostEstimate(
            flops=2 * LAGS * sources * receivers * width,
            bytes_accessed=4 * LAGS * sources * receivers,
            transcendentals=0,
        ),
        name="correlate",
    )(source.reshape(CHUNKS, sources, width // CHUNKS), turned)


def solution(mesh):
    rows, cols = mesh.shape["row"], mesh.shape["col"]
    in_specs = (P(None, ("row", "col"), None), P(), P(), P(("row", "col")))
    out_specs = P(None, "row", "col")
    return jax.shard_map(
        functools.partial(body, rows, cols),
        mesh=mesh,
        in_specs=in_specs,
        out_specs=out_specs,
        check_vma=False,
    )
```

```python
import functools
import math

import jax
import jax.numpy as jnp
from jax import lax
from jax.experimental import pallas as pl
from jax.experimental.pallas import tpu as pltpu
from jax.sharding import PartitionSpec as P

STRIDE = 20
TAPS = 200
HALFWIN = 32
MAXLAG = 25
SUB = 4
LAGS = 51
LANES = 128
BAND_FRAMES = 32
BAND_STEP = BAND_FRAMES * STRIDE
BAND_WIDTH = 896
PARTS = 3
LAG_GROUP = 3
SLOTS = 4
CHUNKS = 2

MESH = pl.DeviceIdType.MESH

def split_parts(values, count):
    parts = []
    for _ in range(count):
        part = values.astype(jnp.bfloat16)
        parts.append(part)
        values = values - part.astype(jnp.float32)
    return parts


def filter_band(tap_row):
    base = jnp.broadcast_to(tap_row, (8, TAPS))
    base = jnp.concatenate([base, jnp.zeros((8, BAND_WIDTH - TAPS), jnp.float32)], axis=1)
    place = lax.broadcasted_iota(jnp.int32, (8, BAND_WIDTH), 0)
    groups = []
    for group in range(BAND_FRAMES // 8):
        held = jnp.zeros((8, BAND_WIDTH), jnp.float32)
        for row in range(8):
            shift = (group * 8 + row) * STRIDE
            moved = base if shift == 0 else pltpu.roll(base, shift, 1)
            held = jnp.where(place == row, moved, held)
        groups.append(held)
    return jnp.concatenate(groups, axis=0)


def nearest_first(cols):
    return [sorted(range(cols), key=lambda other: (abs(other - c), other)) for c in range(cols)]


def whiten_and_send(
    rows, cols, plan_hbm, tap_hbm, quality_hbm, record_ref,
    source_ref, turned_ref,
    receiver_ref, raw, table, plan_ref, tap_ref, quality_ref,
    load_sem, keep_sem, source_sem, receiver_sem, out_sem, plane_sem, twin_sem,
):
    r, c = lax.axis_index("row"), lax.axis_index("col")
    parity = lax.rem(r, 2)
    pair = lax.div(r, 2)
    twin = r + 1 - 2 * parity
    on_diagonal = pair == c
    slots, chans, length = raw.shape
    frames = length // STRIDE
    bits = cols.bit_length() - 1

    loads = [
        pltpu.make_async_copy(tap_hbm, tap_ref, load_sem.at[slots]),
        pltpu.make_async_copy(plan_hbm, plan_ref, load_sem.at[slots + 1]),
        pltpu.make_async_copy(quality_hbm, quality_ref, load_sem.at[slots + 2]),
    ] + [pltpu.make_async_copy(record_ref.at[i], raw.at[i], load_sem.at[i]) for i in range(slots)]
    for load in loads:
        load.start()

    def bit(value, k):
        return lax.rem(lax.div(value, 2**k), 2)

    def across(k):
        return r + 2 * 2**k * (1 - 2 * bit(pair, k))

    def other_core(row):
        return row + 1 - 2 * parity

    barrier = pltpu.get_barrier_semaphore()

    def greet(row, col):
        pl.semaphore_signal(barrier, inc=1, device_id=(row, col), device_id_type=MESH)

    for step in range(1, cols):
        greet(r, lax.rem(c + step, cols))
    for k in range(bits):
        greet(across(k), c)
        greet(other_core(across(k)), c)
    greet(twin, c)

    loads[0].wait()
    band = filter_band(tap_ref[...])
    blocks = frames // BAND_FRAMES
    band = jnp.concatenate([band] * blocks, axis=0).T
    lanes = lax.broadcasted_iota(jnp.int32, (BAND_STEP, frames), 1)
    reach = BAND_WIDTH - BAND_STEP
    for number, part in enumerate(split_parts(band, PARTS)):
        part = part.astype(jnp.float32)
        for block in range(blocks):
            first = block * BAND_FRAMES
            here = jnp.logical_and(lanes >= first, lanes < first + BAND_FRAMES)
            rows = jnp.where(here, part[:BAND_STEP], 0.0)
            if block > 0:
                before = jnp.logical_and(lanes >= first - BAND_FRAMES, lanes < first)
                head = rows[:reach] + jnp.where(before[:reach], part[BAND_STEP:], 0.0)
                rows = jnp.concatenate([head, rows[reach:]], axis=0)
            table[
                block * BAND_STEP : (block + 1) * BAND_STEP,
                number * frames : (number + 1) * frames,
            ] = rows.astype(jnp.bfloat16)

    for load in loads[1:]:
        load.wait()
    picked = jnp.concatenate([raw[plan_ref[s]] for s in range(SUB)], axis=0)
    summed = jnp.dot(picked, table[...], preferred_element_type=jnp.float32)
    decimated = summed[:, :frames]
    for number in range(1, PARTS):
        decimated = decimated + summed[:, number * frames : (number + 1) * frames]

    near = lax.broadcasted_iota(jnp.int32, (frames, frames), 0)
    near = jnp.abs(near - lax.broadcasted_iota(jnp.int32, (frames, frames), 1)) <= HALFWIN
    near = near.astype(jnp.float32).astype(jnp.bfloat16)
    windows = SUB // CHUNKS
    square = lax.broadcasted_iota(jnp.int32, (chans, chans), 0) == lax.broadcasted_iota(
        jnp.int32, (chans, chans), 1
    )
    usable = jnp.broadcast_to(quality_ref[...].astype(jnp.float32), (chans, chans))
    usable = jnp.sum(jnp.where(square, usable, 0.0), axis=1, keepdims=True)

    def whiten(chunk):
        part = decimated[chunk * windows * chans : (chunk + 1) * windows * chans]
        envelope = jnp.zeros_like(part)
        for piece in split_parts(jnp.abs(part), PARTS):
            envelope = envelope + jnp.dot(piece, near, preferred_element_type=jnp.float32)
        scaled = part / (envelope / (2 * HALFWIN + 1) + 1e-05)
        for s in range(windows):
            window = scaled[s * chans : (s + 1) * chans] * usable
            source_ref[chunk, c, :, s * frames : (s + 1) * frames] = window.astype(jnp.bfloat16)

    def remote(src, dst, send_sem, recv_sem, row, col):
        return pltpu.make_async_remote_copy(
            src_ref=src, dst_ref=dst, send_sem=send_sem, recv_sem=recv_sem,
            device_id=(row, col), device_id_type=MESH,
        )

    def along(chunk, step):
        target = lax.rem(pair + step, cols)
        mine = source_ref.at[chunk, c]
        copy = remote(mine, mine, out_sem.at[chunk, step], source_sem.at[chunk, c], r, target)
        return target != c, copy

    def source_arrival(chunk, number):
        block = source_ref.at[chunk, number]
        return remote(
            block, block, out_sem.at[0, 0], source_sem.at[chunk, number],
            r, lax.rem(c + 1, cols),
        )

    half = parity * cols

    def receiver_arrival(chunk, number):
        block = receiver_ref.at[chunk, number]
        return remote(
            block, block, out_sem.at[0, 0], receiver_sem.at[chunk, number], twin, c
        )

    def hand_on(block, chunk, number, to, send_sem):
        return remote(
            block, receiver_ref.at[chunk, half + number], send_sem,
            receiver_sem.at[chunk, half + number], to, c,
        )

    for chunk in range(CHUNKS):
        whiten(chunk)
        if chunk == 0:
            pl.semaphore_wait(barrier, cols - 1 + 2 * bits + 1)
        other, copy = along(chunk, 0)
        pl.when(other)(copy.start)
    for chunk in range(CHUNKS):
        for step in range(1, cols):
            other, copy = along(chunk, step)
            pl.when(other)(copy.start)

    order = nearest_first(cols)

    def place(step):
        number = jnp.int32(order[0][step])
        for column in range(1, cols):
            number = jnp.where(c == column, order[column][step], number)
        return number

    differs = [bit(pair, k) != bit(c, k) for k in range(bits)]
    far = sum(jnp.where(differ, 1, 0) for differ in differs) > 1

    def passes_on(step, k):
        ahead = range(k + 1) if step % 2 == 0 else range(k, bits)
        free = jnp.logical_not(differs[k])
        for other in ahead:
            free = jnp.logical_and(free, jnp.logical_not(differs[other]))
        return free

    def kept(chunk, step):
        number = place(step)
        return pltpu.make_async_copy(
            source_ref.at[chunk, number],
            receiver_ref.at[chunk, half + number],
            keep_sem.at[chunk, step],
        )

    every = [(chunk, step) for chunk in range(CHUNKS) for step in range(cols)]

    @pl.when(on_diagonal)
    def _():
        for chunk, step in every:
            number = place(step)
            if step > 0:
                source_arrival(chunk, number).wait_recv()
            mine = source_ref.at[chunk, number]
            for k in range(bits):
                hand_on(mine, chunk, number, across(k), plane_sem.at[chunk, step, k, 0]).start()
            hand_on(mine, chunk, number, twin, twin_sem.at[chunk, step]).start()
            kept(chunk, step).start()
        for chunk, step in every:
            kept(chunk, step).wait()

    @pl.when(jnp.logical_not(on_diagonal))
    def _():
        for chunk, step in every:
            number = place(step)
            mine = receiver_ref.at[chunk, half + number]
            receiver_arrival(chunk, half + number).wait_recv()
            for k in range(bits):
                sends = passes_on(step, k)
                for core, to in enumerate((across(k), other_core(across(k)))):
                    pl.when(sends)(
                        hand_on(mine, chunk, number, to, plane_sem.at[chunk, step, k, core]).start
                    )
            pl.when(jnp.logical_not(far))(
                hand_on(mine, chunk, number, twin, twin_sem.at[chunk, step]).start
            )
        for chunk, step in every:
            if step > 0:
                source_arrival(chunk, lax.rem(c + step, cols)).wait_recv()

    width = windows * frames
    for chunk in range(CHUNKS):
        for number in range(cols):
            receiver_arrival(chunk, cols - half + number).wait_recv()
        whole = receiver_ref[chunk].reshape(2 * cols * chans, width)
        turned_ref[chunk * width : (chunk + 1) * width, :] = (
            whole.astype(jnp.float32).T.astype(jnp.bfloat16)
        )
    for chunk, step in every:
        other, copy = along(chunk, step)
        pl.when(other)(copy.wait_send)
        block = receiver_ref.at[chunk, half + step]
        for k in range(bits):
            sends = passes_on(step, k)
            pl.when(jnp.logical_or(on_diagonal, sends))(
                hand_on(block, chunk, step, across(k), plane_sem.at[chunk, step, k, 0]).wait_send
            )
            pl.when(jnp.logical_and(jnp.logical_not(on_diagonal), sends))(
                hand_on(block, chunk, step, across(k), plane_sem.at[chunk, step, k, 1]).wait_send
            )
        pl.when(jnp.logical_not(far))(
            hand_on(block, chunk, step, twin, twin_sem.at[chunk, step]).wait_send
        )


def correlate(scale, source_ref, turned, out_ref, even, odd, held, sems):
    frames = LANES
    chunks, sources, width = source_ref.shape
    windows = width // frames
    groups = out_ref.shape[0] // LAG_GROUP
    lane = lax.broadcasted_iota(jnp.int32, (sources, frames), 1)

    def send(group):
        slot = lax.rem(group, SLOTS)
        return pltpu.make_async_copy(
            held.at[slot], out_ref.at[pl.ds(group * LAG_GROUP, LAG_GROUP)], sems.at[slot]
        )

    def send_lag(group, inner):
        slot = lax.rem(group, SLOTS)
        pltpu.make_async_copy(
            held.at[slot, inner], out_ref.at[group * LAG_GROUP + inner], sems.at[slot]
        ).start(priority=inner % 2)

    def fill(moved, group, inner):
        lag = group * LAG_GROUP + inner - MAXLAG
        from_place = lane - lag
        inside = jnp.logical_and(from_place >= 0, from_place < frames)
        shift = lax.rem(lag + frames, frames)
        rows = slice(inner * sources, (inner + 1) * sources)
        for s in range(chunks * windows):
            place = s % windows * frames
            window = pltpu.roll(source_ref[s // windows, :, place : place + frames], shift, 1)
            moved[rows, s * frames : (s + 1) * frames] = jnp.where(inside, window, 0.0).astype(
                jnp.bfloat16
            )

    def multiply(rows):
        return jnp.dot(rows, turned[...], preferred_element_type=jnp.float32) * scale

    def turn(group, now, later):
        slot = lax.rem(group, SLOTS)

        @pl.when(group >= SLOTS)
        def _():
            send(group - SLOTS).wait()

        held[slot] = multiply(now[...]).reshape(held.shape[1:])
        for inner in range(LAG_GROUP):
            fill(later, group + 1, inner)
        for inner in range(LAG_GROUP):
            send_lag(group, inner)

    for inner in range(LAG_GROUP):
        fill(even, 0, inner)
        held[0, inner] = multiply(even[inner * sources : (inner + 1) * sources, :])
        send_lag(0, inner)
    for inner in range(LAG_GROUP):
        fill(odd, 1, inner)

    def step(index, carry):
        turn(2 * index + 1, odd, even)
        turn(2 * index + 2, even, odd)
        return carry

    lax.fori_loop(0, groups // 2, step, 0)
    for group in range(groups - SLOTS, groups):
        send(group).wait()


def body(rows, cols, record, taps, plan, quality):
    slots, chans, length = record.shape
    width = SUB * (length // STRIDE)
    hbm = pl.BlockSpec(memory_space=pltpu.HBM)
    vmem = pl.BlockSpec(memory_space=pltpu.VMEM)
    anywhere = pl.BlockSpec(memory_space=pl.ANY)
    operands = (plan, taps.reshape(1, TAPS), quality.reshape(1, chans), record)
    sources = cols * chans
    receivers = 2 * sources
    bits = cols.bit_length() - 1
    source, turned = pl.pallas_call(
        functools.partial(whiten_and_send, rows, cols),
        out_shape=(
            jax.ShapeDtypeStruct((CHUNKS, cols, chans, width // CHUNKS), jnp.bfloat16),
            jax.ShapeDtypeStruct((width, receivers), jnp.bfloat16),
        ),
        in_specs=[hbm] * 4,
        out_specs=(vmem, vmem),
        scratch_shapes=[
            pltpu.VMEM((CHUNKS, 2 * cols, chans, width // CHUNKS), jnp.bfloat16),
            pltpu.VMEM((slots, chans, length), jnp.bfloat16),
            pltpu.VMEM((length, PARTS * (length // STRIDE)), jnp.bfloat16),
            pltpu.SMEM(plan.shape, jnp.int32),
            pltpu.VMEM((1, TAPS), jnp.float32),
            pltpu.VMEM((1, chans), jnp.int32),
            pltpu.SemaphoreType.DMA((slots + 3,)),
            pltpu.SemaphoreType.DMA((CHUNKS, cols)),
            pltpu.SemaphoreType.DMA((CHUNKS, cols)),
            pltpu.SemaphoreType.DMA((CHUNKS, 2 * cols)),
            pltpu.SemaphoreType.DMA((CHUNKS, cols)),
            pltpu.SemaphoreType.DMA((CHUNKS, cols, bits, 2)),
            pltpu.SemaphoreType.DMA((CHUNKS, cols)),
        ],
        compiler_params=pltpu.CompilerParams(
            collective_id=0, has_side_effects=True, vmem_limit_bytes=32 * 2**20
        ),
        name="whiten_and_send",
    )(*(pltpu.with_memory_space_constraint(held, pltpu.HBM) for held in operands))
    return pl.pallas_call(
        functools.partial(correlate, 1.0 / math.sqrt(width)),
        out_shape=jax.ShapeDtypeStruct((LAGS, sources, receivers), jnp.float32),
        in_specs=[vmem, vmem],
        out_specs=anywhere,
        scratch_shapes=[
            pltpu.VMEM((LAG_GROUP * sources, width), jnp.bfloat16),
            pltpu.VMEM((LAG_GROUP * sources, width), jnp.bfloat16),
            pltpu.VMEM((SLOTS, LAG_GROUP, sources, receivers), jnp.float32),
            pltpu.SemaphoreType.DMA((SLOTS,)),
        ],
        compiler_params=pltpu.CompilerParams(vmem_limit_bytes=32 * 2**20),
        cost_estimate=pl.CostEstimate(
            flops=2 * LAGS * sources * receivers * width,
            bytes_accessed=4 * LAGS * sources * receivers,
            transcendentals=0,
        ),
        name="correlate",
    )(source.reshape(CHUNKS, sources, width // CHUNKS), turned)


def solution(mesh):
    rows, cols = mesh.shape["row"], mesh.shape["col"]
    in_specs = (P(None, ("row", "col"), None), P(), P(), P(("row", "col")))
    out_specs = P(None, "row", "col")
    return jax.shard_map(
        functools.partial(body, rows, cols),
        mesh=mesh,
        in_specs=in_specs,
        out_specs=out_specs,
        check_vma=False,
    )
```

```python
import functools
import math

import jax
import jax.numpy as jnp
from jax import lax
from jax.experimental import pallas as pl
from jax.experimental.pallas import tpu as pltpu
from jax.sharding import PartitionSpec as P

STRIDE = 20
TAPS = 200
HALFWIN = 32
MAXLAG = 25
SUB = 4
LAGS = 51
LANES = 128
BAND_FRAMES = 32
BAND_STEP = BAND_FRAMES * STRIDE
BAND_WIDTH = 896
PARTS = 3
LAG_GROUP = 3
SLOTS = 4
CHUNKS = 4

MESH = pl.DeviceIdType.MESH

def split_parts(values, count):
    parts = []
    for _ in range(count):
        part = values.astype(jnp.bfloat16)
        parts.append(part)
        values = values - part.astype(jnp.float32)
    return parts


def filter_band(tap_row):
    base = jnp.broadcast_to(tap_row, (8, TAPS))
    base = jnp.concatenate([base, jnp.zeros((8, BAND_WIDTH - TAPS), jnp.float32)], axis=1)
    place = lax.broadcasted_iota(jnp.int32, (8, BAND_WIDTH), 0)
    groups = []
    for group in range(BAND_FRAMES // 8):
        held = jnp.zeros((8, BAND_WIDTH), jnp.float32)
        for row in range(8):
            shift = (group * 8 + row) * STRIDE
            moved = base if shift == 0 else pltpu.roll(base, shift, 1)
            held = jnp.where(place == row, moved, held)
        groups.append(held)
    return jnp.concatenate(groups, axis=0)


def nearest_first(cols):
    return [sorted(range(cols), key=lambda other: (abs(other - c), other)) for c in range(cols)]


def whiten_and_send(
    rows, cols, plan_hbm, tap_hbm, quality_hbm, record_ref,
    source_ref, turned_ref,
    receiver_ref, raw, table, plan_ref, tap_ref, quality_ref,
    load_sem, keep_sem, source_sem, receiver_sem, out_sem, plane_sem, twin_sem,
):
    r, c = lax.axis_index("row"), lax.axis_index("col")
    parity = lax.rem(r, 2)
    pair = lax.div(r, 2)
    twin = r + 1 - 2 * parity
    on_diagonal = pair == c
    slots, chans, length = raw.shape
    frames = length // STRIDE
    bits = cols.bit_length() - 1

    loads = [
        pltpu.make_async_copy(tap_hbm, tap_ref, load_sem.at[slots]),
        pltpu.make_async_copy(plan_hbm, plan_ref, load_sem.at[slots + 1]),
        pltpu.make_async_copy(quality_hbm, quality_ref, load_sem.at[slots + 2]),
    ] + [pltpu.make_async_copy(record_ref.at[i], raw.at[i], load_sem.at[i]) for i in range(slots)]
    for load in loads:
        load.start()

    def bit(value, k):
        return lax.rem(lax.div(value, 2**k), 2)

    def across(k):
        return r + 2 * 2**k * (1 - 2 * bit(pair, k))

    def other_core(row):
        return row + 1 - 2 * parity

    barrier = pltpu.get_barrier_semaphore()

    def greet(row, col):
        pl.semaphore_signal(barrier, inc=1, device_id=(row, col), device_id_type=MESH)

    for step in range(1, cols):
        greet(r, lax.rem(c + step, cols))
    for k in range(bits):
        greet(across(k), c)
        greet(other_core(across(k)), c)
    greet(twin, c)

    loads[0].wait()
    band = filter_band(tap_ref[...])
    blocks = frames // BAND_FRAMES
    band = jnp.concatenate([band] * blocks, axis=0).T
    lanes = lax.broadcasted_iota(jnp.int32, (BAND_STEP, frames), 1)
    reach = BAND_WIDTH - BAND_STEP
    for number, part in enumerate(split_parts(band, PARTS)):
        part = part.astype(jnp.float32)
        for block in range(blocks):
            first = block * BAND_FRAMES
            here = jnp.logical_and(lanes >= first, lanes < first + BAND_FRAMES)
            rows = jnp.where(here, part[:BAND_STEP], 0.0)
            if block > 0:
                before = jnp.logical_and(lanes >= first - BAND_FRAMES, lanes < first)
                head = rows[:reach] + jnp.where(before[:reach], part[BAND_STEP:], 0.0)
                rows = jnp.concatenate([head, rows[reach:]], axis=0)
            table[
                block * BAND_STEP : (block + 1) * BAND_STEP,
                number * frames : (number + 1) * frames,
            ] = rows.astype(jnp.bfloat16)

    for load in loads[1:]:
        load.wait()
    picked = jnp.concatenate([raw[plan_ref[s]] for s in range(SUB)], axis=0)
    summed = jnp.dot(picked, table[...], preferred_element_type=jnp.float32)
    decimated = summed[:, :frames]
    for number in range(1, PARTS):
        decimated = decimated + summed[:, number * frames : (number + 1) * frames]

    near = lax.broadcasted_iota(jnp.int32, (frames, frames), 0)
    near = jnp.abs(near - lax.broadcasted_iota(jnp.int32, (frames, frames), 1)) <= HALFWIN
    near = near.astype(jnp.float32).astype(jnp.bfloat16)
    windows = SUB // CHUNKS
    square = lax.broadcasted_iota(jnp.int32, (chans, chans), 0) == lax.broadcasted_iota(
        jnp.int32, (chans, chans), 1
    )
    usable = jnp.broadcast_to(quality_ref[...].astype(jnp.float32), (chans, chans))
    usable = jnp.sum(jnp.where(square, usable, 0.0), axis=1, keepdims=True)

    def whiten(chunk):
        part = decimated[chunk * windows * chans : (chunk + 1) * windows * chans]
        envelope = jnp.zeros_like(part)
        for piece in split_parts(jnp.abs(part), PARTS):
            envelope = envelope + jnp.dot(piece, near, preferred_element_type=jnp.float32)
        scaled = part / (envelope / (2 * HALFWIN + 1) + 1e-05)
        for s in range(windows):
            window = scaled[s * chans : (s + 1) * chans] * usable
            source_ref[chunk, c, :, s * frames : (s + 1) * frames] = window.astype(jnp.bfloat16)

    def remote(src, dst, send_sem, recv_sem, row, col):
        return pltpu.make_async_remote_copy(
            src_ref=src, dst_ref=dst, send_sem=send_sem, recv_sem=recv_sem,
            device_id=(row, col), device_id_type=MESH,
        )

    def along(chunk, step):
        target = lax.rem(pair + step, cols)
        mine = source_ref.at[chunk, c]
        copy = remote(mine, mine, out_sem.at[chunk, step], source_sem.at[chunk, c], r, target)
        return target != c, copy

    def source_arrival(chunk, number):
        block = source_ref.at[chunk, number]
        return remote(
            block, block, out_sem.at[0, 0], source_sem.at[chunk, number],
            r, lax.rem(c + 1, cols),
        )

    half = parity * cols

    def receiver_arrival(chunk, number):
        block = receiver_ref.at[chunk, number]
        return remote(
            block, block, out_sem.at[0, 0], receiver_sem.at[chunk, number], twin, c
        )

    def hand_on(block, chunk, number, to, send_sem):
        return remote(
            block, receiver_ref.at[chunk, half + number], send_sem,
            receiver_sem.at[chunk, half + number], to, c,
        )

    for chunk in range(CHUNKS):
        whiten(chunk)
        if chunk == 0:
            pl.semaphore_wait(barrier, cols - 1 + 2 * bits + 1)
        other, copy = along(chunk, 0)
        pl.when(other)(copy.start)
    for chunk in range(CHUNKS):
        for step in range(1, cols):
            other, copy = along(chunk, step)
            pl.when(other)(copy.start)

    order = nearest_first(cols)

    def place(step):
        number = jnp.int32(order[0][step])
        for column in range(1, cols):
            number = jnp.where(c == column, order[column][step], number)
        return number

    differs = [bit(pair, k) != bit(c, k) for k in range(bits)]
    far = sum(jnp.where(differ, 1, 0) for differ in differs) > 1

    def passes_on(step, k):
        ahead = range(k + 1) if step % 2 == 0 else range(k, bits)
        free = jnp.logical_not(differs[k])
        for other in ahead:
            free = jnp.logical_and(free, jnp.logical_not(differs[other]))
        return free

    def kept(chunk, step):
        number = place(step)
        return pltpu.make_async_copy(
            source_ref.at[chunk, number],
            receiver_ref.at[chunk, half + number],
            keep_sem.at[chunk, step],
        )

    every = [(chunk, step) for chunk in range(CHUNKS) for step in range(cols)]

    @pl.when(on_diagonal)
    def _():
        for chunk, step in every:
            number = place(step)
            if step > 0:
                source_arrival(chunk, number).wait_recv()
            mine = source_ref.at[chunk, number]
            for k in range(bits):
                hand_on(mine, chunk, number, across(k), plane_sem.at[chunk, step, k, 0]).start()
            hand_on(mine, chunk, number, twin, twin_sem.at[chunk, step]).start()
            kept(chunk, step).start()
        for chunk, step in every:
            kept(chunk, step).wait()

    @pl.when(jnp.logical_not(on_diagonal))
    def _():
        for chunk, step in every:
            number = place(step)
            mine = receiver_ref.at[chunk, half + number]
            receiver_arrival(chunk, half + number).wait_recv()
            for k in range(bits):
                sends = passes_on(step, k)
                for core, to in enumerate((across(k), other_core(across(k)))):
                    pl.when(sends)(
                        hand_on(mine, chunk, number, to, plane_sem.at[chunk, step, k, core]).start
                    )
            pl.when(jnp.logical_not(far))(
                hand_on(mine, chunk, number, twin, twin_sem.at[chunk, step]).start
            )
        for chunk, step in every:
            if step > 0:
                source_arrival(chunk, lax.rem(c + step, cols)).wait_recv()

    width = windows * frames
    for chunk in range(CHUNKS):
        for number in range(cols):
            receiver_arrival(chunk, cols - half + number).wait_recv()
        whole = receiver_ref[chunk].reshape(2 * cols * chans, width)
        turned_ref[chunk * width : (chunk + 1) * width, :] = (
            whole.astype(jnp.float32).T.astype(jnp.bfloat16)
        )
    for chunk, step in every:
        other, copy = along(chunk, step)
        pl.when(other)(copy.wait_send)
        block = receiver_ref.at[chunk, half + step]
        for k in range(bits):
            sends = passes_on(step, k)
            pl.when(jnp.logical_or(on_diagonal, sends))(
                hand_on(block, chunk, step, across(k), plane_sem.at[chunk, step, k, 0]).wait_send
            )
            pl.when(jnp.logical_and(jnp.logical_not(on_diagonal), sends))(
                hand_on(block, chunk, step, across(k), plane_sem.at[chunk, step, k, 1]).wait_send
            )
        pl.when(jnp.logical_not(far))(
            hand_on(block, chunk, step, twin, twin_sem.at[chunk, step]).wait_send
        )


def correlate(scale, source_ref, turned, out_ref, even, odd, held, sems):
    frames = LANES
    chunks, sources, width = source_ref.shape
    windows = width // frames
    groups = out_ref.shape[0] // LAG_GROUP
    lane = lax.broadcasted_iota(jnp.int32, (sources, frames), 1)

    def send(group):
        slot = lax.rem(group, SLOTS)
        return pltpu.make_async_copy(
            held.at[slot], out_ref.at[pl.ds(group * LAG_GROUP, LAG_GROUP)], sems.at[slot]
        )

    def send_lag(group, inner):
        slot = lax.rem(group, SLOTS)
        pltpu.make_async_copy(
            held.at[slot, inner], out_ref.at[group * LAG_GROUP + inner], sems.at[slot]
        ).start(priority=inner % 2)

    def fill(moved, group, inner):
        lag = group * LAG_GROUP + inner - MAXLAG
        from_place = lane - lag
        inside = jnp.logical_and(from_place >= 0, from_place < frames)
        shift = lax.rem(lag + frames, frames)
        rows = slice(inner * sources, (inner + 1) * sources)
        for s in range(chunks * windows):
            place = s % windows * frames
            window = pltpu.roll(source_ref[s // windows, :, place : place + frames], shift, 1)
            moved[rows, s * frames : (s + 1) * frames] = jnp.where(inside, window, 0.0).astype(
                jnp.bfloat16
            )

    def multiply(rows):
        return jnp.dot(rows, turned[...], preferred_element_type=jnp.float32) * scale

    def turn(group, now, later):
        slot = lax.rem(group, SLOTS)

        @pl.when(group >= SLOTS)
        def _():
            send(group - SLOTS).wait()

        held[slot] = multiply(now[...]).reshape(held.shape[1:])
        for inner in range(LAG_GROUP):
            fill(later, group + 1, inner)
        for inner in range(LAG_GROUP):
            send_lag(group, inner)

    for inner in range(LAG_GROUP):
        fill(even, 0, inner)
        held[0, inner] = multiply(even[inner * sources : (inner + 1) * sources, :])
        send_lag(0, inner)
    for inner in range(LAG_GROUP):
        fill(odd, 1, inner)

    def step(index, carry):
        turn(2 * index + 1, odd, even)
        turn(2 * index + 2, even, odd)
        return carry

    lax.fori_loop(0, groups // 2, step, 0)
    for group in range(groups - SLOTS, groups):
        send(group).wait()


def body(rows, cols, record, taps, plan, quality):
    slots, chans, length = record.shape
    width = SUB * (length // STRIDE)
    hbm = pl.BlockSpec(memory_space=pltpu.HBM)
    vmem = pl.BlockSpec(memory_space=pltpu.VMEM)
    anywhere = pl.BlockSpec(memory_space=pl.ANY)
    operands = (plan, taps.reshape(1, TAPS), quality.reshape(1, chans), record)
    sources = cols * chans
    receivers = 2 * sources
    bits = cols.bit_length() - 1
    source, turned = pl.pallas_call(
        functools.partial(whiten_and_send, rows, cols),
        out_shape=(
            jax.ShapeDtypeStruct((CHUNKS, cols, chans, width // CHUNKS), jnp.bfloat16),
            jax.ShapeDtypeStruct((width, receivers), jnp.bfloat16),
        ),
        in_specs=[hbm] * 4,
        out_specs=(vmem, vmem),
        scratch_shapes=[
            pltpu.VMEM((CHUNKS, 2 * cols, chans, width // CHUNKS), jnp.bfloat16),
            pltpu.VMEM((slots, chans, length), jnp.bfloat16),
            pltpu.VMEM((length, PARTS * (length // STRIDE)), jnp.bfloat16),
            pltpu.SMEM(plan.shape, jnp.int32),
            pltpu.VMEM((1, TAPS), jnp.float32),
            pltpu.VMEM((1, chans), jnp.int32),
            pltpu.SemaphoreType.DMA((slots + 3,)),
            pltpu.SemaphoreType.DMA((CHUNKS, cols)),
            pltpu.SemaphoreType.DMA((CHUNKS, cols)),
            pltpu.SemaphoreType.DMA((CHUNKS, 2 * cols)),
            pltpu.SemaphoreType.DMA((CHUNKS, cols)),
            pltpu.SemaphoreType.DMA((CHUNKS, cols, bits, 2)),
            pltpu.SemaphoreType.DMA((CHUNKS, cols)),
        ],
        compiler_params=pltpu.CompilerParams(
            collective_id=0, has_side_effects=True, vmem_limit_bytes=32 * 2**20
        ),
        name="whiten_and_send",
    )(*(pltpu.with_memory_space_constraint(held, pltpu.HBM) for held in operands))
    return pl.pallas_call(
        functools.partial(correlate, 1.0 / math.sqrt(width)),
        out_shape=jax.ShapeDtypeStruct((LAGS, sources, receivers), jnp.float32),
        in_specs=[vmem, vmem],
        out_specs=anywhere,
        scratch_shapes=[
            pltpu.VMEM((LAG_GROUP * sources, width), jnp.bfloat16),
            pltpu.VMEM((LAG_GROUP * sources, width), jnp.bfloat16),
            pltpu.VMEM((SLOTS, LAG_GROUP, sources, receivers), jnp.float32),
            pltpu.SemaphoreType.DMA((SLOTS,)),
        ],
        compiler_params=pltpu.CompilerParams(vmem_limit_bytes=32 * 2**20),
        cost_estimate=pl.CostEstimate(
            flops=2 * LAGS * sources * receivers * width,
            bytes_accessed=4 * LAGS * sources * receivers,
            transcendentals=0,
        ),
        name="correlate",
    )(source.reshape(CHUNKS, sources, width // CHUNKS), turned)


def solution(mesh):
    rows, cols = mesh.shape["row"], mesh.shape["col"]
    in_specs = (P(None, ("row", "col"), None), P(), P(), P(("row", "col")))
    out_specs = P(None, "row", "col")
    return jax.shard_map(
        functools.partial(body, rows, cols),
        mesh=mesh,
        in_specs=in_specs,
        out_specs=out_specs,
        check_vma=False,
    )
```

```python
import functools
import math

import jax
import jax.numpy as jnp
from jax import lax
from jax.experimental import pallas as pl
from jax.experimental.pallas import tpu as pltpu
from jax.sharding import PartitionSpec as P

STRIDE = 20
TAPS = 200
HALFWIN = 32
MAXLAG = 25
SUB = 4
LAGS = 51
LANES = 128
BAND_FRAMES = 32
BAND_STEP = BAND_FRAMES * STRIDE
BAND_WIDTH = 896
PARTS = 3
LAG_GROUP = 3
SLOTS = 4
CHUNKS = 4

MESH = pl.DeviceIdType.MESH

def split_parts(values, count):
    parts = []
    for _ in range(count):
        part = values.astype(jnp.bfloat16)
        parts.append(part)
        values = values - part.astype(jnp.float32)
    return parts


def filter_band(tap_row):
    base = jnp.broadcast_to(tap_row, (8, TAPS))
    base = jnp.concatenate([base, jnp.zeros((8, BAND_WIDTH - TAPS), jnp.float32)], axis=1)
    place = lax.broadcasted_iota(jnp.int32, (8, BAND_WIDTH), 0)
    groups = []
    for group in range(BAND_FRAMES // 8):
        held = jnp.zeros((8, BAND_WIDTH), jnp.float32)
        for row in range(8):
            shift = (group * 8 + row) * STRIDE
            moved = base if shift == 0 else pltpu.roll(base, shift, 1)
            held = jnp.where(place == row, moved, held)
        groups.append(held)
    return jnp.concatenate(groups, axis=0)


def nearest_first(cols):
    return [sorted(range(cols), key=lambda other: (abs(other - c), other)) for c in range(cols)]


def whiten_and_send(
    rows, cols, plan_hbm, tap_hbm, quality_hbm, record_ref,
    source_ref, turned_ref,
    receiver_ref, raw, table, plan_ref, tap_ref, quality_ref,
    load_sem, keep_sem, source_sem, receiver_sem, out_sem, plane_sem, twin_sem,
):
    r, c = lax.axis_index("row"), lax.axis_index("col")
    parity = lax.rem(r, 2)
    pair = lax.div(r, 2)
    twin = r + 1 - 2 * parity
    on_diagonal = pair == c
    slots, chans, length = raw.shape
    frames = length // STRIDE
    bits = cols.bit_length() - 1

    loads = [
        pltpu.make_async_copy(tap_hbm, tap_ref, load_sem.at[slots]),
        pltpu.make_async_copy(plan_hbm, plan_ref, load_sem.at[slots + 1]),
        pltpu.make_async_copy(quality_hbm, quality_ref, load_sem.at[slots + 2]),
    ] + [pltpu.make_async_copy(record_ref.at[i], raw.at[i], load_sem.at[i]) for i in range(slots)]
    for load in loads:
        load.start()

    def bit(value, k):
        return lax.rem(lax.div(value, 2**k), 2)

    def across(k):
        return r + 2 * 2**k * (1 - 2 * bit(pair, k))

    barrier = pltpu.get_barrier_semaphore()

    def greet(row, col):
        pl.semaphore_signal(barrier, inc=1, device_id=(row, col), device_id_type=MESH)

    for step in range(1, cols):
        greet(r, lax.rem(c + step, cols))
    for k in range(bits):
        greet(across(k), c)
    greet(twin, c)

    loads[0].wait()
    band = filter_band(tap_ref[...])
    blocks = frames // BAND_FRAMES
    band = jnp.concatenate([band] * blocks, axis=0).T
    lanes = lax.broadcasted_iota(jnp.int32, (BAND_STEP, frames), 1)
    reach = BAND_WIDTH - BAND_STEP
    for number, part in enumerate(split_parts(band, PARTS)):
        part = part.astype(jnp.float32)
        for block in range(blocks):
            first = block * BAND_FRAMES
            here = jnp.logical_and(lanes >= first, lanes < first + BAND_FRAMES)
            rows = jnp.where(here, part[:BAND_STEP], 0.0)
            if block > 0:
                before = jnp.logical_and(lanes >= first - BAND_FRAMES, lanes < first)
                head = rows[:reach] + jnp.where(before[:reach], part[BAND_STEP:], 0.0)
                rows = jnp.concatenate([head, rows[reach:]], axis=0)
            table[
                block * BAND_STEP : (block + 1) * BAND_STEP,
                number * frames : (number + 1) * frames,
            ] = rows.astype(jnp.bfloat16)

    for load in loads[1:]:
        load.wait()
    picked = jnp.concatenate([raw[plan_ref[s]] for s in range(SUB)], axis=0)
    summed = jnp.dot(picked, table[...], preferred_element_type=jnp.float32)
    decimated = summed[:, :frames]
    for number in range(1, PARTS):
        decimated = decimated + summed[:, number * frames : (number + 1) * frames]

    near = lax.broadcasted_iota(jnp.int32, (frames, frames), 0)
    near = jnp.abs(near - lax.broadcasted_iota(jnp.int32, (frames, frames), 1)) <= HALFWIN
    near = near.astype(jnp.float32).astype(jnp.bfloat16)
    windows = SUB // CHUNKS
    square = lax.broadcasted_iota(jnp.int32, (chans, chans), 0) == lax.broadcasted_iota(
        jnp.int32, (chans, chans), 1
    )
    usable = jnp.broadcast_to(quality_ref[...].astype(jnp.float32), (chans, chans))
    usable = jnp.sum(jnp.where(square, usable, 0.0), axis=1, keepdims=True)

    def whiten(chunk):
        part = decimated[chunk * windows * chans : (chunk + 1) * windows * chans]
        envelope = jnp.zeros_like(part)
        for piece in split_parts(jnp.abs(part), PARTS):
            envelope = envelope + jnp.dot(piece, near, preferred_element_type=jnp.float32)
        scaled = part / (envelope / (2 * HALFWIN + 1) + 1e-05)
        for s in range(windows):
            window = scaled[s * chans : (s + 1) * chans] * usable
            source_ref[chunk, c, :, s * frames : (s + 1) * frames] = window.astype(jnp.bfloat16)

    def remote(src, dst, send_sem, recv_sem, row, col):
        return pltpu.make_async_remote_copy(
            src_ref=src, dst_ref=dst, send_sem=send_sem, recv_sem=recv_sem,
            device_id=(row, col), device_id_type=MESH,
        )

    def along(chunk, step):
        target = lax.rem(pair + step, cols)
        mine = source_ref.at[chunk, c]
        copy = remote(mine, mine, out_sem.at[chunk, step], source_sem.at[chunk, c], r, target)
        return target != c, copy

    def source_arrival(chunk, number):
        block = source_ref.at[chunk, number]
        return remote(
            block, block, out_sem.at[0, 0], source_sem.at[chunk, number],
            r, lax.rem(c + 1, cols),
        )

    half = parity * cols

    def receiver_arrival(chunk, number):
        block = receiver_ref.at[chunk, number]
        return remote(
            block, block, out_sem.at[0, 0], receiver_sem.at[chunk, number], twin, c
        )

    def hand_on(block, chunk, number, to, send_sem):
        return remote(
            block, receiver_ref.at[chunk, half + number], send_sem,
            receiver_sem.at[chunk, half + number], to, c,
        )

    for chunk in range(CHUNKS):
        whiten(chunk)
        if chunk == 0:
            pl.semaphore_wait(barrier, cols - 1 + bits + 1)
        other, copy = along(chunk, 0)
        pl.when(other)(copy.start)
    for chunk in range(CHUNKS):
        for step in range(1, cols):
            other, copy = along(chunk, step)
            pl.when(other)(copy.start)

    order = nearest_first(cols)

    def place(step):
        number = jnp.int32(order[0][step])
        for column in range(1, cols):
            number = jnp.where(c == column, order[column][step], number)
        return number

    differs = [bit(pair, k) != bit(c, k) for k in range(bits)]

    def passes_on(step, k):
        ahead = range(k + 1) if step % 2 == 0 else range(k, bits)
        free = jnp.logical_not(differs[k])
        for other in ahead:
            free = jnp.logical_and(free, jnp.logical_not(differs[other]))
        return free

    def kept(chunk, step):
        number = place(step)
        return pltpu.make_async_copy(
            source_ref.at[chunk, number],
            receiver_ref.at[chunk, half + number],
            keep_sem.at[chunk, step],
        )

    every = [(chunk, step) for chunk in range(CHUNKS) for step in range(cols)]

    @pl.when(on_diagonal)
    def _():
        for chunk, step in every:
            number = place(step)
            if step > 0:
                source_arrival(chunk, number).wait_recv()
            mine = source_ref.at[chunk, number]
            for k in range(bits):
                hand_on(mine, chunk, number, across(k), plane_sem.at[chunk, step, k, 0]).start()
            hand_on(mine, chunk, number, twin, twin_sem.at[chunk, step]).start()
            kept(chunk, step).start()
        for chunk, step in every:
            kept(chunk, step).wait()

    @pl.when(jnp.logical_not(on_diagonal))
    def _():
        for chunk, step in every:
            number = place(step)
            mine = receiver_ref.at[chunk, half + number]
            receiver_arrival(chunk, half + number).wait_recv()
            for k in range(bits):
                sends = passes_on(step, k)
                pl.when(sends)(
                    hand_on(mine, chunk, number, across(k), plane_sem.at[chunk, step, k, 0]).start
                )
            hand_on(mine, chunk, number, twin, twin_sem.at[chunk, step]).start()
        for chunk, step in every:
            if step > 0:
                source_arrival(chunk, lax.rem(c + step, cols)).wait_recv()

    width = windows * frames
    for chunk in range(CHUNKS):
        for number in range(cols):
            receiver_arrival(chunk, cols - half + number).wait_recv()
        whole = receiver_ref[chunk].reshape(2 * cols * chans, width)
        turned_ref[chunk * width : (chunk + 1) * width, :] = (
            whole.astype(jnp.float32).T.astype(jnp.bfloat16)
        )
    for chunk, step in every:
        other, copy = along(chunk, step)
        pl.when(other)(copy.wait_send)
        block = receiver_ref.at[chunk, half + step]
        for k in range(bits):
            sends = passes_on(step, k)
            pl.when(jnp.logical_or(on_diagonal, sends))(
                hand_on(block, chunk, step, across(k), plane_sem.at[chunk, step, k, 0]).wait_send
            )
        hand_on(block, chunk, step, twin, twin_sem.at[chunk, step]).wait_send()


def correlate(scale, source_ref, turned, out_ref, even, odd, held, sems):
    frames = LANES
    chunks, sources, width = source_ref.shape
    windows = width // frames
    groups = out_ref.shape[0] // LAG_GROUP
    lane = lax.broadcasted_iota(jnp.int32, (sources, frames), 1)

    def send(group):
        slot = lax.rem(group, SLOTS)
        return pltpu.make_async_copy(
            held.at[slot], out_ref.at[pl.ds(group * LAG_GROUP, LAG_GROUP)], sems.at[slot]
        )

    def send_lag(group, inner):
        slot = lax.rem(group, SLOTS)
        pltpu.make_async_copy(
            held.at[slot, inner], out_ref.at[group * LAG_GROUP + inner], sems.at[slot]
        ).start(priority=inner % 2)

    def fill(moved, group, inner):
        lag = group * LAG_GROUP + inner - MAXLAG
        from_place = lane - lag
        inside = jnp.logical_and(from_place >= 0, from_place < frames)
        shift = lax.rem(lag + frames, frames)
        rows = slice(inner * sources, (inner + 1) * sources)
        for s in range(chunks * windows):
            place = s % windows * frames
            window = pltpu.roll(source_ref[s // windows, :, place : place + frames], shift, 1)
            moved[rows, s * frames : (s + 1) * frames] = jnp.where(inside, window, 0.0).astype(
                jnp.bfloat16
            )

    def multiply(rows):
        return jnp.dot(rows, turned[...], preferred_element_type=jnp.float32) * scale

    def turn(group, now, later):
        slot = lax.rem(group, SLOTS)

        @pl.when(group >= SLOTS)
        def _():
            send(group - SLOTS).wait()

        held[slot] = multiply(now[...]).reshape(held.shape[1:])
        for inner in range(LAG_GROUP):
            fill(later, group + 1, inner)
        for inner in range(LAG_GROUP):
            send_lag(group, inner)

    for inner in range(LAG_GROUP):
        fill(even, 0, inner)
        held[0, inner] = multiply(even[inner * sources : (inner + 1) * sources, :])
        send_lag(0, inner)
    for inner in range(LAG_GROUP):
        fill(odd, 1, inner)

    def step(index, carry):
        turn(2 * index + 1, odd, even)
        turn(2 * index + 2, even, odd)
        return carry

    lax.fori_loop(0, groups // 2, step, 0)
    for group in range(groups - SLOTS, groups):
        send(group).wait()


def body(rows, cols, record, taps, plan, quality):
    slots, chans, length = record.shape
    width = SUB * (length // STRIDE)
    hbm = pl.BlockSpec(memory_space=pltpu.HBM)
    vmem = pl.BlockSpec(memory_space=pltpu.VMEM)
    anywhere = pl.BlockSpec(memory_space=pl.ANY)
    operands = (plan, taps.reshape(1, TAPS), quality.reshape(1, chans), record)
    sources = cols * chans
    receivers = 2 * sources
    bits = cols.bit_length() - 1
    source, turned = pl.pallas_call(
        functools.partial(whiten_and_send, rows, cols),
        out_shape=(
            jax.ShapeDtypeStruct((CHUNKS, cols, chans, width // CHUNKS), jnp.bfloat16),
            jax.ShapeDtypeStruct((width, receivers), jnp.bfloat16),
        ),
        in_specs=[hbm] * 4,
        out_specs=(vmem, vmem),
        scratch_shapes=[
            pltpu.VMEM((CHUNKS, 2 * cols, chans, width // CHUNKS), jnp.bfloat16),
            pltpu.VMEM((slots, chans, length), jnp.bfloat16),
            pltpu.VMEM((length, PARTS * (length // STRIDE)), jnp.bfloat16),
            pltpu.SMEM(plan.shape, jnp.int32),
            pltpu.VMEM((1, TAPS), jnp.float32),
            pltpu.VMEM((1, chans), jnp.int32),
            pltpu.SemaphoreType.DMA((slots + 3,)),
            pltpu.SemaphoreType.DMA((CHUNKS, cols)),
            pltpu.SemaphoreType.DMA((CHUNKS, cols)),
            pltpu.SemaphoreType.DMA((CHUNKS, 2 * cols)),
            pltpu.SemaphoreType.DMA((CHUNKS, cols)),
            pltpu.SemaphoreType.DMA((CHUNKS, cols, bits, 1)),
            pltpu.SemaphoreType.DMA((CHUNKS, cols)),
        ],
        compiler_params=pltpu.CompilerParams(
            collective_id=0, has_side_effects=True, vmem_limit_bytes=32 * 2**20
        ),
        name="whiten_and_send",
    )(*(pltpu.with_memory_space_constraint(held, pltpu.HBM) for held in operands))
    return pl.pallas_call(
        functools.partial(correlate, 1.0 / math.sqrt(width)),
        out_shape=jax.ShapeDtypeStruct((LAGS, sources, receivers), jnp.float32),
        in_specs=[vmem, vmem],
        out_specs=anywhere,
        scratch_shapes=[
            pltpu.VMEM((LAG_GROUP * sources, width), jnp.bfloat16),
            pltpu.VMEM((LAG_GROUP * sources, width), jnp.bfloat16),
            pltpu.VMEM((SLOTS, LAG_GROUP, sources, receivers), jnp.float32),
            pltpu.SemaphoreType.DMA((SLOTS,)),
        ],
        compiler_params=pltpu.CompilerParams(vmem_limit_bytes=32 * 2**20),
        cost_estimate=pl.CostEstimate(
            flops=2 * LAGS * sources * receivers * width,
            bytes_accessed=4 * LAGS * sources * receivers,
            transcendentals=0,
        ),
        name="correlate",
    )(source.reshape(CHUNKS, sources, width // CHUNKS), turned)


def solution(mesh):
    rows, cols = mesh.shape["row"], mesh.shape["col"]
    in_specs = (P(None, ("row", "col"), None), P(), P(), P(("row", "col")))
    out_specs = P(None, "row", "col")
    return jax.shard_map(
        functools.partial(body, rows, cols),
        mesh=mesh,
        in_specs=in_specs,
        out_specs=out_specs,
        check_vma=False,
    )
```
